32 devices in a mesh: parts: 2 (over x), wide: 16 (over z, y, core).
Axes of the slice: x: 2, y: 2, z: 4, core: 2. Of those that a mesh axis runs over, the one named last changes fastest.
Arguments:
- hidden_in: bfloat16 [64, 8192], P(('parts', 'wide')), parts along dimension 0, may hold values from -6 to 6
- queries: bfloat16 [64, 8192], P(('parts', 'wide')), parts along dimension 0, may hold values from -6 to 6
- key_new: bfloat16 [64, 1024], P(('parts', 'wide')), parts along dimension 0, may hold values from -6 to 6
- value_new: bfloat16 [64, 1024], P(('parts', 'wide')), parts along dimension 0, may hold values from -6 to 6
- key_cache: bfloat16 [4096, 1024], P(('parts', 'wide')), parts along dimension 0, may hold values from -6 to 6
- value_cache: bfloat16 [4096, 1024], P(('parts', 'wide')), parts along dimension 0, may hold values from -6 to 6
- lengths: int32 [32], P(('parts', 'wide')), parts along dimension 0, may hold values from 1 to 128, as said below
- table: int32 [32, 1], P('parts'), parts along dimension 0, may hold values from 0 to 1; in each aligned block of 16 rows (0 to 15, 16 to 31, ...) at most 12 rows name the same one
- gain: float32 [8192], replicated, may hold values from 0.25 to 1.75
- gate_weight: bfloat16 [8192, 4096], P(None, 'wide'), may hold values from -0.0625 to 0.0625
- up_weight: bfloat16 [8192, 4096], P(None, 'wide'), may hold values from -0.0625 to 0.0625
- down_weight: bfloat16 [4096, 8192], P('wide'), may hold values from -0.25 to 0.25
Outputs:
- mixed: bfloat16 [64, 8192], P(('parts', 'wide')), parts along dimension 0
The draws below stay inside these ranges and needn't reach their ends.
There are 2 independent parts, one for each index of `parts`. The reference program is written for one: setup_inputs(seed, part) draws one part's arguments, and reference() takes and returns one part's arrays. A program takes and returns all parts, laid end to end along the dimension named above; an argument that names none is the same for every part. Nothing has to cross between parts.
Inputs may be any that keep to these rules, and one draw needn't show every extreme that they name: `lengths`: at least one prompt has all 128 cached positions valid. `table`: no group serves more than 12 prompts, and one group serves exactly 12.
All inputs are finite; a program needn't handle non-finite values.
Results may differ from the reference program's by a relative error of at most 0.0067.
Values may be sent and summed in bfloat16 or wider, within the bound.
No kernel may reach another device: no remote copies, remote signals or barrier semaphores. Data moves between devices by JAX's collectives and lax.ppermute only.
A program may use at most 64 MiB of HBM per device.

```python
import math
import jax
import jax.numpy as jnp
import numpy as np
from jax import lax

D = 8192
HEADS = 64
KV_HEADS = 8
HEAD = 128
FF_DEV = 256
GROUPS = 2
ROWS = 2
CACHE = 128
CAP = 12
FF = 4096
N_WIDE = 16


def draw_lengths(key, part):
    key = jax.random.fold_in(key, 11)
    values = jax.random.randint(key, (N_WIDE,), 1, CACHE + 1)
    chosen = jax.random.randint(jax.random.fold_in(key, 5), (), 0, N_WIDE)
    return values.at[chosen].set(CACHE).astype(jnp.int32)


def draw_hidden_in(key, part):
    key = jax.random.fold_in(key, 31)
    total_rows = N_WIDE * ROWS
    values = jnp.clip(jax.random.normal(key, (total_rows, D), jnp.float32), -6.0, 6.0)
    return values.astype(jnp.bfloat16)


def draw_queries(key, part):
    key = jax.random.fold_in(key, 21)
    total_rows = N_WIDE * ROWS
    values = jnp.clip(jax.random.normal(key, (total_rows, D), jnp.float32), -6.0, 6.0)
    return values.astype(jnp.bfloat16)


def draw_key_new(key, part):
    key = jax.random.fold_in(key, 22)
    total_rows = N_WIDE * ROWS
    columns = KV_HEADS * HEAD
    values = jnp.clip(jax.random.normal(key, (total_rows, columns), jnp.float32), -6.0, 6.0)
    return values.astype(jnp.bfloat16)


def levels(key, dims, cuts, low, high):
    level = 1.0
    for axis_at, parts in cuts:
        steps = jax.random.uniform(jax.random.fold_in(jax.random.fold_in(key, 6), axis_at), (parts,), jnp.float32, low / len(cuts), high / len(cuts))
        level = level * jnp.repeat(jnp.exp(steps), dims[axis_at] // parts).reshape((-1,) + (1,) * (len(dims) - 1 - axis_at))
    return level


def deal_out(stream_key, own, number, rows, count, top, bound, lean):
    order = jax.random.permutation(stream_key, count)
    crowded, ordinary = load_shares(count, rows * top, bound, lean, True), load_shares(count, rows * top, bound, lean, False)
    places = jnp.arange(count)

    def named(sizes, offset_by):
        used = int((sizes > 0).sum())
        fixed = max(1, used // 4)
        shifted = fixed + (places - fixed + offset_by * (used - fixed)) % max(1, count - fixed)
        return jnp.zeros((count,), jnp.int32).at[order[jnp.where(places < fixed, places, shifted)]].set(jnp.asarray(sizes, jnp.int32))

    sizes = jnp.where(number % 4 == 0, named(crowded, number // 4), named(ordinary, number - number // 4 - 1))
    mixed = jax.random.permutation(jax.random.fold_in(own, 3), count)
    donor, receiver = mixed[0:count // 2 * 2:2], mixed[1:count // 2 * 2:2]
    margin = jnp.minimum(sizes[donor] - 1, bound - sizes[receiver]) // 2
    margin = jnp.where((donor == order[0]) | (receiver == order[0]) | (sizes[receiver] == 0), 0, jnp.maximum(margin, 0))
    shifted = jax.random.randint(jax.random.fold_in(own, 4), (count // 2,), 0, 1 << 20) % (margin + 1)
    sizes = sizes.at[donor].add(-shifted).at[receiver].add(shifted)
    members = jnp.searchsorted(jnp.cumsum(sizes), jnp.arange(rows * top), side="right").astype(jnp.int32)
    listing = members.reshape(top, rows).T
    listing = listing[jax.random.permutation(jax.random.fold_in(own, 1), rows)]
    offset_by = jax.random.randint(jax.random.fold_in(own, 2), (rows, 1), 0, top)
    return jnp.take_along_axis(listing, (jnp.arange(top)[None, :] + offset_by) % top, axis=1)


def load_shares(number_of, total, bound, slope, full):
    portions = [(1 << 20) // math.isqrt(rank ** slope) + 1 for rank in range(1, number_of + 1)]
    largest = bound if full else min(bound, max(-(-total // number_of), total * portions[0] // sum(portions)))
    least = 1 if total - largest >= number_of - 1 else 0
    holding, surplus = [largest] + [least] * (number_of - 1), total - largest - least * (number_of - 1)
    while surplus > 0:
        free = [i for i in range(1, number_of) if holding[i] < largest] or [i for i in range(1, number_of) if holding[i] < bound]
        mass, budget = sum([portions[i] for i in free]), surplus
        for i in free:
            more = min(bound - holding[i], max(1, budget * portions[i] // mass), surplus)
            holding[i] = holding[i] + more
            surplus = surplus - more
    return np.array(holding)


def scatter_about(key, dims, deviation, bound, cuts=(), kind=jnp.bfloat16):
    loudness = levels(key, dims, cuts, -0.22, 0.18) if cuts else 1.0
    array = jax.random.normal(key, dims, jnp.float32) * deviation * loudness
    return jnp.minimum(jnp.maximum(array, -bound), bound).astype(kind)


def setup_inputs(seed: int = 0, part: int = 0) -> dict:
    key_list = jax.random.split(jax.random.key(seed), 13)
    part_keys = jax.random.split(jax.random.fold_in(key_list[12], part), 13)
    hidden_in = draw_hidden_in(jax.random.fold_in(jax.random.fold_in(key_list[12], part), 71), part)
    queries = draw_queries(jax.random.fold_in(jax.random.fold_in(key_list[12], part), 71), part)
    key_new = draw_key_new(jax.random.fold_in(jax.random.fold_in(key_list[12], part), 71), part)
    value_new = scatter_about(part_keys[3], (N_WIDE * ROWS, KV_HEADS * HEAD), 1.0, 6.0, ((0, 16),))
    key_cache = scatter_about(part_keys[4], (N_WIDE * CACHE, KV_HEADS * HEAD), 1.0, 6.0, ((0, 16),))
    value_cache = scatter_about(part_keys[5], (N_WIDE * CACHE, KV_HEADS * HEAD), 1.0, 6.0, ((0, 16),))
    lengths = draw_lengths(jax.random.fold_in(jax.random.fold_in(key_list[12], part), 71), part)
    table_keys = jax.random.split(jax.random.fold_in(part_keys[7], 1), N_WIDE // N_WIDE)
    table_turns = jax.random.permutation(jax.random.fold_in(part_keys[7], 3), N_WIDE // N_WIDE)
    table = jax.vmap(lambda own, number: deal_out(jax.random.fold_in(part_keys[7], 2), own, number, N_WIDE, GROUPS, 1, CAP, 2))(table_keys, table_turns).reshape((N_WIDE, 1))
    gain = jnp.clip(1.0 + 0.15 * jax.random.normal(key_list[8], (D,), jnp.float32), 0.25, 1.75)
    gate_weight = scatter_about(key_list[9], (D, FF), D ** -0.5, 0.0625, ((1, 16),))
    up_weight = scatter_about(key_list[10], (D, FF), D ** -0.5, 0.0625, ((1, 16),))
    down_weight = scatter_about(key_list[11], (FF, D), (FF_DEV * N_WIDE // (4 * GROUPS)) ** -0.5, 0.25, ((0, 16),))
    return dict(hidden_in=hidden_in, queries=queries, key_new=key_new, value_new=value_new, key_cache=key_cache, value_cache=value_cache, lengths=lengths, table=table, gain=gain, gate_weight=gate_weight, up_weight=up_weight, down_weight=down_weight)


def attend_prompt(query_rows, key_all, value_all, length):
    rows = query_rows.shape[0]
    ratio = HEADS // KV_HEADS
    query_heads = query_rows.astype(jnp.float32).reshape(rows, KV_HEADS, ratio, HEAD)
    key_heads = key_all.astype(jnp.float32).reshape(-1, KV_HEADS, HEAD)
    value_heads = value_all.astype(jnp.float32).reshape(-1, KV_HEADS, HEAD)
    scores = jnp.einsum('rkgh,jkh->kgrj', query_heads, key_heads) / jnp.sqrt(jnp.float32(HEAD))
    key_index = jnp.arange(CACHE + rows, dtype=jnp.int32)[None, :]
    row_index = jnp.arange(rows, dtype=jnp.int32)[:, None]
    visible = jnp.where(key_index < CACHE, key_index < length, key_index - CACHE <= row_index)
    scores = jnp.where(visible, scores, jnp.float32(-1e+30))
    top = lax.optimization_barrier(jnp.max(scores, axis=-1, keepdims=True))
    raised = jnp.exp(scores - top)
    probs = (raised / lax.optimization_barrier(jnp.sum(raised, axis=-1, keepdims=True))).astype(jnp.bfloat16)
    probs = lax.optimization_barrier(probs).astype(jnp.float32)
    context = jnp.einsum('kgrj,jkh->rkgh', probs, value_heads)
    return context.reshape(rows, HEAD * HEADS).astype(jnp.bfloat16)

def reference(hidden_in, queries, key_new, value_new, key_cache, value_cache, lengths, table, gain, gate_weight, up_weight, down_weight):
    width = lengths.shape[0]

    def one_prompt(index):
        query_rows = lax.dynamic_slice_in_dim(queries, index * ROWS, ROWS, 0)
        key_all = jnp.concatenate([lax.dynamic_slice_in_dim(key_cache, index * CACHE, CACHE, 0), lax.dynamic_slice_in_dim(key_new, index * ROWS, ROWS, 0)], 0)
        value_all = jnp.concatenate([lax.dynamic_slice_in_dim(value_cache, index * CACHE, CACHE, 0), lax.dynamic_slice_in_dim(value_new, index * ROWS, ROWS, 0)], 0)
        context = attend_prompt(query_rows, key_all, value_all, lengths[index])
        context = lax.optimization_barrier(context).astype(jnp.float32)
        own_rows = lax.dynamic_slice_in_dim(hidden_in, index * ROWS, ROWS, 0)
        return own_rows.astype(jnp.float32) + context
    resid = lax.map(one_prompt, jnp.arange(width, dtype=jnp.int32)).reshape(width * ROWS, D)
    normed = (resid * lax.rsqrt(lax.optimization_barrier(jnp.mean(resid * resid, axis=-1, keepdims=True)) + 1e-05) * gain).astype(jnp.bfloat16)
    owner_rows = jnp.repeat(table[:, 0], ROWS)
    group_width = gate_weight.shape[1] // GROUPS
    ffn_sum = jnp.zeros((width * ROWS, D), jnp.float32)
    for group in range(GROUPS):
        low = group * group_width
        high = low + group_width
        gate = jnp.dot(normed, gate_weight[:, low:high], preferred_element_type=jnp.float32)
        upper = jnp.dot(normed, up_weight[:, low:high], preferred_element_type=jnp.float32)
        hidden = (jax.nn.silu(gate) * upper).astype(jnp.bfloat16)
        partial_value = jnp.dot(hidden, down_weight[low:high], preferred_element_type=jnp.float32)
        ffn_sum = jnp.where((owner_rows == group)[:, None], partial_value, ffn_sum)
    ffn_out = lax.optimization_barrier(ffn_sum.astype(jnp.bfloat16)).astype(jnp.float32)
    return (resid + ffn_out).astype(jnp.bfloat16)
```

```python
import functools

import jax
import jax.numpy as jnp
from jax import lax
from jax.experimental import pallas as pl
from jax.experimental.pallas import tpu as pltpu
from jax.sharding import PartitionSpec as P

HEADS = 64
KV_HEADS = 8
HEAD = 128
GROUPS = 2
F32 = jnp.float32
BF16 = jnp.bfloat16
VMEM = pltpu.VMEM
SMEM = pltpu.SMEM


def attend_kernel(rows, len_ref, hid_ref, q_ref, kn_ref, vn_ref, kc_ref, vc_ref, gain_ref, normed_ref, resid_ref, wide_gain):
    total = q_ref.shape[0]
    part = total // KV_HEADS
    cached = kc_ref.shape[0]
    for r in range(rows):
        wide_gain[pl.ds(r, total // rows, stride=rows), :] = gain_ref[...]
    scale = HEAD ** -0.5
    scores = jnp.concatenate(
        [
            lax.dot_general(
                q_ref[k * part : (k + 1) * part, :],
                kc_ref[:, k * HEAD : (k + 1) * HEAD],
                (((1,), (1,)), ((), ())),
                preferred_element_type=F32,
            )
            for k in range(KV_HEADS)
        ],
        0,
    ) * scale
    seen = lax.broadcasted_iota(jnp.int32, (total, cached), 1) < len_ref[0]
    scores = jnp.where(seen, scores, -1e30)
    turn = lax.broadcasted_iota(jnp.int32, (total, 1), 0) % rows
    query = q_ref[...].astype(F32)
    fresh = []
    values = []
    for t in range(rows):
        keys = jnp.concatenate(
            [
                jnp.broadcast_to(kn_ref[t : t + 1, k * HEAD : (k + 1) * HEAD].astype(F32), (part, HEAD))
                for k in range(KV_HEADS)
            ],
            0,
        )
        score = jnp.sum(query * keys, axis=1, keepdims=True) * scale
        fresh.append(jnp.where(turn >= t, score, -1e30))
        values.append(
            jnp.concatenate(
                [
                    jnp.broadcast_to(vn_ref[t : t + 1, k * HEAD : (k + 1) * HEAD].astype(F32), (part, HEAD))
                    for k in range(KV_HEADS)
                ],
                0,
            )
        )
    top = jnp.max(scores, axis=1, keepdims=True)
    for score in fresh:
        top = jnp.maximum(top, score)
    raised = jnp.exp(scores - top)
    bottom = jnp.sum(raised, axis=1, keepdims=True)
    lifted = [jnp.exp(score - top) for score in fresh]
    for value in lifted:
        bottom = bottom + value
    probs = (raised / bottom).astype(BF16)
    context = jnp.concatenate(
        [
            jnp.dot(
                probs[k * part : (k + 1) * part, :],
                vc_ref[:, k * HEAD : (k + 1) * HEAD],
                preferred_element_type=F32,
            )
            for k in range(KV_HEADS)
        ],
        0,
    )
    for value, column in zip(lifted, values):
        context = context + (value / bottom).astype(BF16).astype(F32) * column
    resid = hid_ref[...].astype(F32) + context.astype(BF16).astype(F32)
    resid_ref[...] = resid
    square = jnp.sum(resid * resid, axis=1, keepdims=True)
    factor = jnp.zeros((total, 1), F32)
    width = total // rows * HEAD
    for r in range(rows):
        mean = jnp.sum(jnp.where(turn == r, square, 0.0), axis=0, keepdims=True) / width
        factor = jnp.where(turn == r, lax.rsqrt(mean + 1e-05), factor)
    normed_ref[...] = (resid * factor * wide_gain[...]).astype(BF16)


def attend(rows, lengths, hidden, query, key_new, value_new, key_cache, value_cache, gain):
    vmem = pl.BlockSpec(memory_space=VMEM)
    return pl.pallas_call(
        functools.partial(attend_kernel, rows),
        out_shape=(
            jax.ShapeDtypeStruct(hidden.shape, BF16),
            jax.ShapeDtypeStruct(hidden.shape, F32),
        ),
        in_specs=[pl.BlockSpec(memory_space=SMEM)] + [vmem] * 7,
        out_specs=(vmem, vmem),
        scratch_shapes=[VMEM(hidden.shape, F32)],
        name="attend",
    )(lengths, hidden, query, key_new, value_new, key_cache, value_cache, gain)


CHUNK = 1024


def feed_kernel(x_ref, keep_ref, gate_ref, up_ref, down_ref, out_ref):
    rows, depth = x_ref.shape
    units = gate_ref.shape[1]
    gate = jnp.zeros((rows, units), F32)
    upper = jnp.zeros((rows, units), F32)
    for at in range(0, depth, CHUNK):
        block = x_ref[:, at : at + CHUNK]
        gate += jnp.dot(block, gate_ref[at : at + CHUNK, :], preferred_element_type=F32)
        upper += jnp.dot(block, up_ref[at : at + CHUNK, :], preferred_element_type=F32)
    hidden = gate / (1.0 + jnp.exp(-gate)) * upper
    hidden = jnp.where(keep_ref[...] > 0, hidden, 0.0).astype(BF16)
    for at in range(0, depth, CHUNK):
        out_ref[:, at : at + CHUNK] = jnp.dot(
            hidden, down_ref[:, at : at + CHUNK], preferred_element_type=F32
        ).astype(BF16)


def feed(x, keep, gate_weight, up_weight, down_weight):
    vmem = pl.BlockSpec(memory_space=VMEM)
    weights = [pltpu.with_memory_space_constraint(w, VMEM) for w in (gate_weight, up_weight, down_weight)]
    rows, depth = x.shape
    units = gate_weight.shape[1]
    return pl.pallas_call(
        feed_kernel,
        out_shape=jax.ShapeDtypeStruct(x.shape, BF16),
        in_specs=[vmem] * 5,
        out_specs=vmem,
        compiler_params=pltpu.CompilerParams(vmem_limit_bytes=24 << 20),
        cost_estimate=pl.CostEstimate(
            flops=6 * rows * depth * units, bytes_accessed=6 * depth * units, transcendentals=rows * units
        ),
        name="feed",
    )(x, keep, *weights)


def swap(x, bits, width):
    return lax.ppermute(x, "wide", [(i, i ^ bits) for i in range(width)])


def local(
    hidden_in,
    queries,
    key_new,
    value_new,
    key_cache,
    value_cache,
    lengths,
    table,
    gain,
    gate_weight,
    up_weight,
    down_weight,
):
    rows, depth = hidden_in.shape
    blocks = depth // HEAD
    width = lax.axis_size("wide")
    members = width // GROUPS
    chips = members // 2
    me = lax.axis_index("wide")

    def pairs(x):
        return x.reshape(rows, blocks, HEAD).transpose(1, 0, 2).reshape(rows * blocks, HEAD)

    normed, resid = attend(
        rows,
        lengths,
        pairs(hidden_in),
        pairs(queries),
        key_new,
        value_new,
        key_cache,
        value_cache,
        gain.reshape(blocks, HEAD),
    )
    both = jnp.stack([normed, swap(normed, members, width)], 0)
    mine = jnp.stack([both] + [swap(both, 2 * k, width) for k in range(1, chips)], 0)
    every = jnp.stack([mine, swap(mine, 1, width)], 0)
    code = (
        lax.broadcasted_iota(jnp.int32, (2, chips, 2), 0)
        + 2 * lax.broadcasted_iota(jnp.int32, (2, chips, 2), 1)
        + members * lax.broadcasted_iota(jnp.int32, (2, chips, 2), 2)
    ).reshape(width)
    source = jnp.repeat(me ^ code, rows)
    owners = table[:, 0]
    keep = jnp.any(
        (source[:, None] == lax.iota(jnp.int32, width)[None, :]) & (owners == me // members)[None, :],
        axis=1,
        keepdims=True,
    ).astype(jnp.int32)
    x = every.reshape(width, blocks, rows, HEAD).transpose(0, 2, 1, 3).reshape(width * rows, depth)
    part = feed(x, keep, gate_weight, up_weight, down_weight)
    half = width * rows // 2
    summed = part[:half].astype(F32) + swap(part[half:], 1, width).astype(F32)
    summed = summed.astype(BF16).reshape(chips, 2, rows, blocks, HEAD).transpose(0, 1, 3, 2, 4)
    summed = summed.reshape(chips, 2, rows * blocks, HEAD)
    came = [swap(summed[k], 2 * k, width) for k in range(1, chips)]
    total = summed[0].astype(F32)
    for block in came:
        total = total + block.astype(F32)
    other = swap(total[1].astype(BF16), members, width)
    ffn_out = (total[0] + other.astype(F32)).astype(BF16).astype(F32)
    mixed = (resid + ffn_out).astype(BF16)
    return mixed.reshape(blocks, rows, HEAD).transpose(1, 0, 2).reshape(rows, depth)


def solution(mesh):
    in_specs = (
        P(("parts", "wide"), None),
        P(("parts", "wide"), None),
        P(("parts", "wide"), None),
        P(("parts", "wide"), None),
        P(("parts", "wide"), None),
        P(("parts", "wide"), None),
        P(("parts", "wide")),
        P("parts", None),
        P(),
        P(None, "wide"),
        P(None, "wide"),
        P("wide", None),
    )
    out_specs = P(("parts", "wide"), None)
    return jax.shard_map(local, mesh=mesh, in_specs=in_specs, out_specs=out_specs, check_vma=False)
```

```python
import functools

import jax
import jax.numpy as jnp
from jax import lax
from jax.experimental import pallas as pl
from jax.experimental.pallas import tpu as pltpu
from jax.sharding import PartitionSpec as P

HEADS = 64
KV_HEADS = 8
HEAD = 128
GROUPS = 2
F32 = jnp.float32
BF16 = jnp.bfloat16
VMEM = pltpu.VMEM
SMEM = pltpu.SMEM


def attend_kernel(rows, len_ref, hid_ref, q_ref, kn_ref, vn_ref, kc_ref, vc_ref, gain_ref, normed_ref, resid_ref, wide_gain):
    total = q_ref.shape[0]
    part = total // KV_HEADS
    cached = kc_ref.shape[0]
    for r in range(rows):
        wide_gain[pl.ds(r, total // rows, stride=rows), :] = gain_ref[...]
    scale = HEAD ** -0.5
    scores = jnp.concatenate(
        [
            lax.dot_general(
                q_ref[k * part : (k + 1) * part, :],
                kc_ref[:, k * HEAD : (k + 1) * HEAD],
                (((1,), (1,)), ((), ())),
                preferred_element_type=F32,
            )
            for k in range(KV_HEADS)
        ],
        0,
    ) * scale
    seen = lax.broadcasted_iota(jnp.int32, (total, cached), 1) < len_ref[0]
    scores = jnp.where(seen, scores, -1e30)
    turn = lax.broadcasted_iota(jnp.int32, (total, 1), 0) % rows
    query = q_ref[...].astype(F32)
    fresh = []
    values = []
    for t in range(rows):
        keys = jnp.concatenate(
            [
                jnp.broadcast_to(kn_ref[t : t + 1, k * HEAD : (k + 1) * HEAD].astype(F32), (part, HEAD))
                for k in range(KV_HEADS)
            ],
            0,
        )
        score = jnp.sum(query * keys, axis=1, keepdims=True) * scale
        fresh.append(jnp.where(turn >= t, score, -1e30))
        values.append(
            jnp.concatenate(
                [
                    jnp.broadcast_to(vn_ref[t : t + 1, k * HEAD : (k + 1) * HEAD].astype(F32), (part, HEAD))
                    for k in range(KV_HEADS)
                ],
                0,
            )
        )
    top = jnp.max(scores, axis=1, keepdims=True)
    for score in fresh:
        top = jnp.maximum(top, score)
    raised = jnp.exp(scores - top)
    bottom = jnp.sum(raised, axis=1, keepdims=True)
    lifted = [jnp.exp(score - top) for score in fresh]
    for value in lifted:
        bottom = bottom + value
    probs = (raised / bottom).astype(BF16)
    context = jnp.concatenate(
        [
            jnp.dot(
                probs[k * part : (k + 1) * part, :],
                vc_ref[:, k * HEAD : (k + 1) * HEAD],
                preferred_element_type=F32,
            )
            for k in range(KV_HEADS)
        ],
        0,
    )
    for value, column in zip(lifted, values):
        context = context + (value / bottom).astype(BF16).astype(F32) * column
    resid = hid_ref[...].astype(F32) + context.astype(BF16).astype(F32)
    resid_ref[...] = resid
    square = jnp.sum(resid * resid, axis=1, keepdims=True)
    factor = jnp.zeros((total, 1), F32)
    width = total // rows * HEAD
    for r in range(rows):
        mean = jnp.sum(jnp.where(turn == r, square, 0.0), axis=0, keepdims=True) / width
        factor = jnp.where(turn == r, lax.rsqrt(mean + 1e-05), factor)
    normed_ref[...] = (resid * factor * wide_gain[...]).astype(BF16)


def attend(rows, lengths, hidden, query, key_new, value_new, key_cache, value_cache, gain):
    vmem = pl.BlockSpec(memory_space=VMEM)
    return pl.pallas_call(
        functools.partial(attend_kernel, rows),
        out_shape=(
            VMEM(hidden.shape, BF16),
            VMEM(hidden.shape, F32),
        ),
        in_specs=[pl.BlockSpec(memory_space=SMEM)] + [vmem] * 7,
        out_specs=(vmem, vmem),
        scratch_shapes=[VMEM(hidden.shape, F32)],
        name="attend",
    )(lengths, hidden, query, key_new, value_new, key_cache, value_cache, gain)


FETCHES = 4


def fetch_kernel(count, carry_ref, *refs):
    sources, passed_ref, targets, sems = refs[:count], refs[count], refs[count + 1 : -1], refs[-1]
    copies = []
    for which in range(count):
        size = sources[which].shape[0] // FETCHES
        for i in range(FETCHES):
            span = pl.ds(i * size, size)
            copies.append(
                pltpu.make_async_copy(
                    sources[which].at[span, :], targets[which].at[span, :], sems.at[which * FETCHES + i]
                )
            )
            copies[-1].start()
    passed_ref[...] = carry_ref[...]
    for copy in copies:
        copy.wait()


def fetch(carry, *weights):
    vmem = pl.BlockSpec(memory_space=VMEM)
    count = len(weights)
    return pl.pallas_call(
        functools.partial(fetch_kernel, count),
        out_shape=tuple(VMEM(a.shape, a.dtype) for a in (carry, *weights)),
        in_specs=[vmem] + [pl.BlockSpec(memory_space=pltpu.HBM)] * count,
        out_specs=(vmem,) * (count + 1),
        scratch_shapes=[pltpu.SemaphoreType.DMA((count * FETCHES,))],
        cost_estimate=pl.CostEstimate(
            flops=0, bytes_accessed=sum(4 * w.size for w in weights), transcendentals=0
        ),
        compiler_params=pltpu.CompilerParams(vmem_limit_bytes=4 << 20),
        name="fetch",
    )(carry, *[pltpu.with_memory_space_constraint(w, pltpu.HBM) for w in weights])


CHUNK = 1024


def feed_kernel(new, x_ref, table_ref, gate_ref, up_ref, down_ref, out_ref):
    rows, depth = x_ref.shape
    width = rows // new
    members = width // GROUPS
    me = lax.axis_index("wide")
    block = lax.broadcasted_iota(jnp.int32, (rows, width), 0) // new
    source = me ^ (block // members + block % members // GROUPS * 2 + block % GROUPS * members)
    column = lax.broadcasted_iota(jnp.int32, (rows, width), 1)
    served = (source == column) & (table_ref[...] == me // members)
    keep = jnp.sum(served.astype(jnp.int32), axis=1, keepdims=True) > 0
    units = gate_ref.shape[1]
    gate = jnp.zeros((rows, units), F32)
    upper = jnp.zeros((rows, units), F32)
    for at in range(0, depth, CHUNK):
        block = x_ref[:, at : at + CHUNK]
        gate += jnp.dot(block, gate_ref[at : at + CHUNK, :], preferred_element_type=F32)
        upper += jnp.dot(block, up_ref[at : at + CHUNK, :], preferred_element_type=F32)
    hidden = gate / (1.0 + jnp.exp(-gate)) * upper
    hidden = jnp.where(keep, hidden, 0.0).astype(BF16)
    for at in range(0, depth, CHUNK):
        out_ref[:, at : at + CHUNK] = jnp.dot(
            hidden, down_ref[:, at : at + CHUNK], preferred_element_type=F32
        ).astype(BF16)


def feed(new, x, table, gate_weight, up_weight, down_weight):
    vmem = pl.BlockSpec(memory_space=VMEM)
    weights = [pltpu.with_memory_space_constraint(w, VMEM) for w in (gate_weight, up_weight, down_weight)]
    rows, depth = x.shape
    units = gate_weight.shape[1]
    return pl.pallas_call(
        functools.partial(feed_kernel, new),
        out_shape=jax.ShapeDtypeStruct(x.shape, BF16),
        in_specs=[vmem] * 5,
        out_specs=vmem,
        compiler_params=pltpu.CompilerParams(vmem_limit_bytes=24 << 20),
        cost_estimate=pl.CostEstimate(
            flops=6 * rows * depth * units, bytes_accessed=6 * depth * units, transcendentals=rows * units
        ),
        name="feed",
    )(x, table, *weights)


def swap(x, bits, width):
    return lax.ppermute(x, "wide", [(i, i ^ bits) for i in range(width)])


def local(
    hidden_in,
    queries,
    key_new,
    value_new,
    key_cache,
    value_cache,
    lengths,
    table,
    gain,
    gate_weight,
    up_weight,
    down_weight,
):
    rows, depth = hidden_in.shape
    blocks = depth // HEAD
    width = lax.axis_size("wide")
    members = width // GROUPS
    chips = members // 2

    def pairs(x):
        return x.reshape(rows, blocks, HEAD).transpose(1, 0, 2).reshape(rows * blocks, HEAD)

    normed, resid = attend(
        rows,
        lengths,
        pairs(hidden_in),
        pairs(queries),
        key_new,
        value_new,
        key_cache,
        value_cache,
        gain.reshape(blocks, HEAD),
    )
    twin = swap(normed, members, width)
    normed, gate_weight = fetch(normed, gate_weight)
    both = jnp.stack([normed, twin], 0)
    kept, up_weight, down_weight = fetch(both, up_weight, down_weight)
    mine = jnp.stack([kept] + [swap(both, 2 * k, width) for k in range(1, chips)], 0)
    every = jnp.stack([mine, swap(mine, 1, width)], 0)
    x = every.reshape(width, blocks, rows, HEAD).transpose(0, 2, 1, 3).reshape(width * rows, depth)
    part = feed(rows, x, table.reshape(1, width), gate_weight, up_weight, down_weight)
    half = width * rows // 2
    summed = part[:half].astype(F32) + swap(part[half:], 1, width).astype(F32)
    summed = summed.astype(BF16).reshape(chips, 2, rows, blocks, HEAD).transpose(0, 1, 3, 2, 4)
    summed = summed.reshape(chips, 2, rows * blocks, HEAD)
    came = [swap(summed[k], 2 * k, width) for k in range(1, chips)]
    total = summed[0].astype(F32)
    for block in came:
        total = total + block.astype(F32)
    other = swap(total[1].astype(BF16), members, width)
    ffn_out = (total[0] + other.astype(F32)).astype(BF16).astype(F32)
    mixed = (resid + ffn_out).astype(BF16)
    return mixed.reshape(blocks, rows, HEAD).transpose(1, 0, 2).reshape(rows, depth)


def solution(mesh):
    in_specs = (
        P(("parts", "wide"), None),
        P(("parts", "wide"), None),
        P(("parts", "wide"), None),
        P(("parts", "wide"), None),
        P(("parts", "wide"), None),
        P(("parts", "wide"), None),
        P(("parts", "wide")),
        P("parts", None),
        P(),
        P(None, "wide"),
        P(None, "wide"),
        P("wide", None),
    )
    out_specs = P(("parts", "wide"), None)
    return jax.shard_map(local, mesh=mesh, in_specs=in_specs, out_specs=out_specs, check_vma=False)
```

```python
import functools

import jax
import jax.numpy as jnp
from jax import lax
from jax.experimental import pallas as pl
from jax.experimental.pallas import tpu as pltpu
from jax.sharding import PartitionSpec as P

HEADS = 64
KV_HEADS = 8
HEAD = 128
GROUPS = 2
F32 = jnp.float32
BF16 = jnp.bfloat16
VMEM = pltpu.VMEM
SMEM = pltpu.SMEM


def attend_kernel(rows, len_ref, hid_ref, q_ref, kn_ref, vn_ref, kc_ref, vc_ref, gain_ref, normed_ref, resid_ref, wide_gain, length, sem):
    copy = pltpu.make_async_copy(len_ref, length, sem)
    copy.start()
    total = q_ref.shape[0]
    part = total // KV_HEADS
    cached = kc_ref.shape[0]
    for r in range(rows):
        wide_gain[pl.ds(r, total // rows, stride=rows), :] = gain_ref[...]
    scale = HEAD ** -0.5
    scores = jnp.concatenate(
        [
            lax.dot_general(
                q_ref[k * part : (k + 1) * part, :],
                kc_ref[:, k * HEAD : (k + 1) * HEAD],
                (((1,), (1,)), ((), ())),
                preferred_element_type=F32,
            )
            for k in range(KV_HEADS)
        ],
        0,
    ) * scale
    copy.wait()
    seen = lax.broadcasted_iota(jnp.int32, (total, cached), 1) < length[0]
    scores = jnp.where(seen, scores, -1e30)
    turn = lax.broadcasted_iota(jnp.int32, (total, 1), 0) % rows
    query = q_ref[...].astype(F32)
    fresh = []
    values = []
    for t in range(rows):
        keys = jnp.concatenate(
            [
                jnp.broadcast_to(kn_ref[t : t + 1, k * HEAD : (k + 1) * HEAD].astype(F32), (part, HEAD))
                for k in range(KV_HEADS)
            ],
            0,
        )
        score = jnp.sum(query * keys, axis=1, keepdims=True) * scale
        fresh.append(jnp.where(turn >= t, score, -1e30))
        values.append(
            jnp.concatenate(
                [
                    jnp.broadcast_to(vn_ref[t : t + 1, k * HEAD : (k + 1) * HEAD].astype(F32), (part, HEAD))
                    for k in range(KV_HEADS)
                ],
                0,
            )
        )
    top = jnp.max(scores, axis=1, keepdims=True)
    for score in fresh:
        top = jnp.maximum(top, score)
    raised = jnp.exp(scores - top)
    bottom = jnp.sum(raised, axis=1, keepdims=True)
    lifted = [jnp.exp(score - top) for score in fresh]
    for value in lifted:
        bottom = bottom + value
    probs = (raised / bottom).astype(BF16)
    context = jnp.concatenate(
        [
            jnp.dot(
                probs[k * part : (k + 1) * part, :],
                vc_ref[:, k * HEAD : (k + 1) * HEAD],
                preferred_element_type=F32,
            )
            for k in range(KV_HEADS)
        ],
        0,
    )
    for value, column in zip(lifted, values):
        context = context + (value / bottom).astype(BF16).astype(F32) * column
    resid = hid_ref[...].astype(F32) + context.astype(BF16).astype(F32)
    resid_ref[...] = resid
    square = jnp.sum(resid * resid, axis=1, keepdims=True)
    factor = jnp.zeros((total, 1), F32)
    width = total // rows * HEAD
    for r in range(rows):
        mean = jnp.sum(jnp.where(turn == r, square, 0.0), axis=0, keepdims=True) / width
        factor = jnp.where(turn == r, lax.rsqrt(mean + 1e-05), factor)
    normed_ref[...] = (resid * factor * wide_gain[...]).astype(BF16)


def attend(rows, lengths, hidden, query, key_new, value_new, key_cache, value_cache, gain):
    vmem = pl.BlockSpec(memory_space=VMEM)
    return pl.pallas_call(
        functools.partial(attend_kernel, rows),
        out_shape=(
            VMEM(hidden.shape, BF16),
            VMEM(hidden.shape, F32),
        ),
        in_specs=[pl.BlockSpec(memory_space=pl.ANY)] + [vmem] * 7,
        out_specs=(vmem, vmem),
        scratch_shapes=[VMEM(hidden.shape, F32), SMEM((1,), jnp.int32), pltpu.SemaphoreType.DMA],
        name="attend",
    )(lengths, hidden, query, key_new, value_new, key_cache, value_cache, gain)


FETCHES = 4


def fetch_kernel(count, after_ref, carry_ref, *refs):
    sources, passed_ref, targets, sems = refs[:count], refs[count], refs[count + 1 : -1], refs[-1]
    copies = []
    for which in range(count):
        size = sources[which].shape[0] // FETCHES
        for i in range(FETCHES):
            span = pl.ds(i * size, size)
            copies.append(
                pltpu.make_async_copy(
                    sources[which].at[span, :], targets[which].at[span, :], sems.at[which * FETCHES + i]
                )
            )
            copies[-1].start()
    passed_ref[...] = carry_ref[...]
    for copy in copies:
        copy.wait()


def fetch(after, carry, *weights):
    vmem = pl.BlockSpec(memory_space=VMEM)
    count = len(weights)
    return pl.pallas_call(
        functools.partial(fetch_kernel, count),
        out_shape=tuple(VMEM(a.shape, a.dtype) for a in (carry, *weights)),
        in_specs=[pl.BlockSpec(memory_space=pl.ANY), vmem] + [pl.BlockSpec(memory_space=pltpu.HBM)] * count,
        out_specs=(vmem,) * (count + 1),
        scratch_shapes=[pltpu.SemaphoreType.DMA((count * FETCHES,))],
        cost_estimate=pl.CostEstimate(
            flops=0, bytes_accessed=sum(4 * w.size for w in weights), transcendentals=0
        ),
        compiler_params=pltpu.CompilerParams(vmem_limit_bytes=4 << 20),
        name="fetch",
    )(after, carry, *[pltpu.with_memory_space_constraint(w, pltpu.HBM) for w in weights])


def join_kernel(*refs):
    for at, ref in enumerate(refs[:-1]):
        refs[-1][at] = ref[...]


def join(parts):
    vmem = pl.BlockSpec(memory_space=VMEM)
    return pl.pallas_call(
        join_kernel,
        out_shape=VMEM((len(parts), *parts[0].shape), parts[0].dtype),
        in_specs=[vmem] * len(parts),
        out_specs=vmem,
        compiler_params=pltpu.CompilerParams(vmem_limit_bytes=4 << 20),
        name="join",
    )(*parts)


CHUNK = 1024


def feed_kernel(new, mine_ref, other_ref, table_ref, gate_ref, up_ref, down_ref, keep_ref, send_ref):
    half, depth = mine_ref.shape
    rows = 2 * half
    width = rows // new
    members = width // GROUPS
    me = lax.axis_index("wide")
    block = lax.broadcasted_iota(jnp.int32, (rows, width), 0) // new
    chips = members // 2
    source = me ^ (block // members + block % members // chips * members + block % chips * 2)
    column = lax.broadcasted_iota(jnp.int32, (rows, width), 1)
    served = (source == column) & (table_ref[...] == me // members)
    keep = jnp.sum(served.astype(jnp.int32), axis=1, keepdims=True) > 0
    units = gate_ref.shape[1]
    gate = jnp.zeros((rows, units), F32)
    upper = jnp.zeros((rows, units), F32)
    for at in range(0, depth, CHUNK):
        block = jnp.concatenate([mine_ref[:, at : at + CHUNK], other_ref[:, at : at + CHUNK]], 0)
        gate += jnp.dot(block, gate_ref[at : at + CHUNK, :], preferred_element_type=F32)
        upper += jnp.dot(block, up_ref[at : at + CHUNK, :], preferred_element_type=F32)
    hidden = gate / (1.0 + jnp.exp(-gate)) * upper
    hidden = jnp.where(keep, hidden, 0.0).astype(BF16)
    for at in range(0, depth, CHUNK):
        out = jnp.dot(hidden, down_ref[:, at : at + CHUNK], preferred_element_type=F32).astype(BF16)
        keep_ref[:, at : at + CHUNK] = out[:half]
        send_ref[:, at : at + CHUNK] = out[half:]


def feed(new, mine, other, table, gate_weight, up_weight, down_weight):
    vmem = pl.BlockSpec(memory_space=VMEM)
    weights = [pltpu.with_memory_space_constraint(w, VMEM) for w in (gate_weight, up_weight, down_weight)]
    rows, depth = mine.shape
    units = gate_weight.shape[1]
    return pl.pallas_call(
        functools.partial(feed_kernel, new),
        out_shape=(VMEM(mine.shape, BF16),) * 2,
        in_specs=[vmem] * 6,
        out_specs=(vmem,) * 2,
        compiler_params=pltpu.CompilerParams(vmem_limit_bytes=24 << 20),
        cost_estimate=pl.CostEstimate(
            flops=12 * rows * depth * units, bytes_accessed=6 * depth * units, transcendentals=rows * units
        ),
        name="feed",
    )(mine, other, table, *weights)


def swap(x, bits, width):
    return lax.ppermute(x, "wide", [(i, i ^ bits) for i in range(width)])


def local(
    hidden_in,
    queries,
    key_new,
    value_new,
    key_cache,
    value_cache,
    lengths,
    table,
    gain,
    gate_weight,
    up_weight,
    down_weight,
):
    rows, depth = hidden_in.shape
    blocks = depth // HEAD
    width = lax.axis_size("wide")
    members = width // GROUPS
    chips = members // 2

    def pairs(x):
        return x.reshape(rows, blocks, HEAD).transpose(1, 0, 2).reshape(rows * blocks, HEAD)

    normed, resid = attend(
        rows,
        lengths,
        pairs(hidden_in),
        pairs(queries),
        key_new,
        value_new,
        key_cache,
        value_cache,
        gain.reshape(blocks, HEAD),
    )
    twin = swap(normed, members, width)
    own = [normed] + [swap(normed, 2 * k, width) for k in range(1, chips)]
    twins = [twin] + [swap(twin, 2 * k, width) for k in range(1, chips)]
    twins[0], gate_weight, up_weight = fetch(twin, twin, gate_weight, up_weight)
    mine = join(own + twins)
    mine = mine.reshape(members, blocks, rows, HEAD).transpose(0, 2, 1, 3).reshape(members * rows, depth)
    other = swap(mine, 1, width)
    mine, down_weight = fetch(mine, mine, down_weight)
    kept, sent = feed(rows, mine, other, table.reshape(1, width), gate_weight, up_weight, down_weight)
    summed = kept.astype(F32) + swap(sent, 1, width).astype(F32)
    half = chips * rows

    def gather(first):
        total = summed[first : first + rows]
        for k in range(1, chips):
            at = first + k * rows
            total = total + swap(summed[at : at + rows].astype(BF16), 2 * k, width).astype(F32)
        return total

    other = swap(gather(half).astype(BF16), members, width)
    ffn_out = (gather(0) + other.astype(F32)).astype(BF16).astype(F32)
    resid = resid.reshape(blocks, rows, HEAD).transpose(1, 0, 2).reshape(rows, depth)
    return (resid + ffn_out).astype(BF16)


def solution(mesh):
    in_specs = (
        P(("parts", "wide"), None),
        P(("parts", "wide"), None),
        P(("parts", "wide"), None),
        P(("parts", "wide"), None),
        P(("parts", "wide"), None),
        P(("parts", "wide"), None),
        P(("parts", "wide")),
        P("parts", None),
        P(),
        P(None, "wide"),
        P(None, "wide"),
        P("wide", None),
    )
    out_specs = P(("parts", "wide"), None)
    return jax.shard_map(local, mesh=mesh, in_specs=in_specs, out_specs=out_specs, check_vma=False)
```

```python
import functools

import jax
import jax.numpy as jnp
from jax import lax
from jax.experimental import pallas as pl
from jax.experimental.pallas import tpu as pltpu
from jax.sharding import PartitionSpec as P

HEADS = 64
KV_HEADS = 8
HEAD = 128
GROUPS = 2
F32 = jnp.float32
BF16 = jnp.bfloat16
VMEM = pltpu.VMEM
SMEM = pltpu.SMEM


def attend_kernel(rows, len_ref, hid_ref, q_ref, kn_ref, vn_ref, kc_ref, vc_ref, gain_ref, normed_ref, resid_ref, wide_gain):
    total = q_ref.shape[0]
    part = total // KV_HEADS
    cached = kc_ref.shape[0]
    for r in range(rows):
        wide_gain[pl.ds(r, total // rows, stride=rows), :] = gain_ref[...]
    scale = HEAD ** -0.5
    scores = jnp.concatenate(
        [
            lax.dot_general(
                q_ref[k * part : (k + 1) * part, :],
                kc_ref[:, k * HEAD : (k + 1) * HEAD],
                (((1,), (1,)), ((), ())),
                preferred_element_type=F32,
            )
            for k in range(KV_HEADS)
        ],
        0,
    ) * scale
    seen = lax.broadcasted_iota(jnp.int32, (total, cached), 1) < len_ref[0]
    scores = jnp.where(seen, scores, -1e30)
    turn = lax.broadcasted_iota(jnp.int32, (total, 1), 0) % rows
    query = q_ref[...].astype(F32)
    fresh = []
    values = []
    for t in range(rows):
        keys = jnp.concatenate(
            [
                jnp.broadcast_to(kn_ref[t : t + 1, k * HEAD : (k + 1) * HEAD].astype(F32), (part, HEAD))
                for k in range(KV_HEADS)
            ],
            0,
        )
        score = jnp.sum(query * keys, axis=1, keepdims=True) * scale
        fresh.append(jnp.where(turn >= t, score, -1e30))
        values.append(
            jnp.concatenate(
                [
                    jnp.broadcast_to(vn_ref[t : t + 1, k * HEAD : (k + 1) * HEAD].astype(F32), (part, HEAD))
                    for k in range(KV_HEADS)
                ],
                0,
            )
        )
    top = jnp.max(scores, axis=1, keepdims=True)
    for score in fresh:
        top = jnp.maximum(top, score)
    raised = jnp.exp(scores - top)
    bottom = jnp.sum(raised, axis=1, keepdims=True)
    lifted = [jnp.exp(score - top) for score in fresh]
    for value in lifted:
        bottom = bottom + value
    probs = (raised / bottom).astype(BF16)
    context = jnp.concatenate(
        [
            jnp.dot(
                probs[k * part : (k + 1) * part, :],
                vc_ref[:, k * HEAD : (k + 1) * HEAD],
                preferred_element_type=F32,
            )
            for k in range(KV_HEADS)
        ],
        0,
    )
    for value, column in zip(lifted, values):
        context = context + (value / bottom).astype(BF16).astype(F32) * column
    resid = hid_ref[...].astype(F32) + context.astype(BF16).astype(F32)
    resid_ref[...] = resid
    square = jnp.sum(resid * resid, axis=1, keepdims=True)
    factor = jnp.zeros((total, 1), F32)
    width = total // rows * HEAD
    for r in range(rows):
        mean = jnp.sum(jnp.where(turn == r, square, 0.0), axis=0, keepdims=True) / width
        factor = jnp.where(turn == r, lax.rsqrt(mean + 1e-05), factor)
    normed_ref[...] = (resid * factor * wide_gain[...]).astype(BF16)


def attend(rows, lengths, hidden, query, key_new, value_new, key_cache, value_cache, gain):
    vmem = pl.BlockSpec(memory_space=VMEM)
    return pl.pallas_call(
        functools.partial(attend_kernel, rows),
        out_shape=(
            VMEM(hidden.shape, BF16),
            VMEM(hidden.shape, F32),
        ),
        in_specs=[pl.BlockSpec(memory_space=SMEM)] + [vmem] * 7,
        out_specs=(vmem, vmem),
        scratch_shapes=[VMEM(hidden.shape, F32)],
        name="attend",
    )(lengths, hidden, query, key_new, value_new, key_cache, value_cache, gain)


FETCHES = 4


def fetch_kernel(count, after_ref, carry_ref, *refs):
    sources, passed_ref, targets, sems = refs[:count], refs[count], refs[count + 1 : -1], refs[-1]
    copies = []
    for which in range(count):
        size = sources[which].shape[0] // FETCHES
        for i in range(FETCHES):
            span = pl.ds(i * size, size)
            copies.append(
                pltpu.make_async_copy(
                    sources[which].at[span, :], targets[which].at[span, :], sems.at[which * FETCHES + i]
                )
            )
            copies[-1].start()
    passed_ref[...] = carry_ref[...]
    for copy in copies:
        copy.wait()


def fetch(after, carry, *weights):
    vmem = pl.BlockSpec(memory_space=VMEM)
    count = len(weights)
    return pl.pallas_call(
        functools.partial(fetch_kernel, count),
        out_shape=tuple(VMEM(a.shape, a.dtype) for a in (carry, *weights)),
        in_specs=[pl.BlockSpec(memory_space=pl.ANY), vmem] + [pl.BlockSpec(memory_space=pltpu.HBM)] * count,
        out_specs=(vmem,) * (count + 1),
        scratch_shapes=[pltpu.SemaphoreType.DMA((count * FETCHES,))],
        cost_estimate=pl.CostEstimate(
            flops=0, bytes_accessed=sum(4 * w.size for w in weights), transcendentals=0
        ),
        compiler_params=pltpu.CompilerParams(vmem_limit_bytes=4 << 20),
        name="fetch",
    )(after, carry, *[pltpu.with_memory_space_constraint(w, pltpu.HBM) for w in weights])


def join_kernel(*refs):
    for at, ref in enumerate(refs[:-1]):
        refs[-1][:, at] = ref[...]


def join(parts):
    vmem = pl.BlockSpec(memory_space=VMEM)
    return pl.pallas_call(
        join_kernel,
        out_shape=VMEM((parts[0].shape[0], len(parts), *parts[0].shape[1:]), parts[0].dtype),
        in_specs=[vmem] * len(parts),
        out_specs=vmem,
        compiler_params=pltpu.CompilerParams(vmem_limit_bytes=4 << 20),
        name="join",
    )(*parts)


CHUNK = 1024


def hidden_rows(new, width, first, x_ref, table_ref, gate_ref, up_ref):
    rows, depth = x_ref.shape
    units = gate_ref.shape[1]
    gate = jnp.zeros((rows, units), F32)
    upper = jnp.zeros((rows, units), F32)
    for at in range(0, depth, CHUNK):
        block = x_ref[:, at : at + CHUNK]
        gate += jnp.dot(block, gate_ref[at : at + CHUNK, :], preferred_element_type=F32)
        upper += jnp.dot(block, up_ref[at : at + CHUNK, :], preferred_element_type=F32)
    hidden = gate / (1.0 + jnp.exp(-gate)) * upper
    members = width // GROUPS
    chips = members // 2
    me = lax.axis_index("wide")
    block = first + lax.broadcasted_iota(jnp.int32, (rows, width), 0) // new
    source = me ^ (block // members + block % members // chips * members + block % chips * 2)
    column = lax.broadcasted_iota(jnp.int32, (rows, width), 1)
    served = (source == column) & (table_ref[...] == me // members)
    keep = jnp.sum(served.astype(jnp.int32), axis=1, keepdims=True) > 0
    return jnp.where(keep, hidden, 0.0).astype(BF16)


def down_rows(hidden, down_ref, out_ref):
    for at in range(0, out_ref.shape[1], CHUNK):
        out_ref[:, at : at + CHUNK] = jnp.dot(
            hidden, down_ref[:, at : at + CHUNK], preferred_element_type=F32
        ).astype(BF16)


def hidden_kernel(new, width, first, x_ref, table_ref, gate_ref, up_ref, out_ref):
    out_ref[...] = hidden_rows(new, width, first, x_ref, table_ref, gate_ref, up_ref)


def feed_kernel(new, width, first, after_ref, x_ref, table_ref, gate_ref, up_ref, down_ref, out_ref):
    down_rows(hidden_rows(new, width, first, x_ref, table_ref, gate_ref, up_ref), down_ref, out_ref)


def down_kernel(after_ref, hidden_ref, down_ref, out_ref):
    down_rows(hidden_ref[...], down_ref, out_ref)


def here(kernel, out_shape, products, name, *operands):
    vmem = pl.BlockSpec(memory_space=VMEM)
    return pl.pallas_call(
        kernel,
        out_shape=VMEM(out_shape, BF16),
        in_specs=[vmem] * len(operands),
        out_specs=vmem,
        compiler_params=pltpu.CompilerParams(vmem_limit_bytes=16 << 20),
        cost_estimate=pl.CostEstimate(flops=2 * products, bytes_accessed=4 << 20, transcendentals=0),
        name=name,
    )(*[pltpu.with_memory_space_constraint(x, VMEM) for x in operands])


def swap(x, bits, width):
    return lax.ppermute(x, "wide", [(i, i ^ bits) for i in range(width)])


def local(
    hidden_in,
    queries,
    key_new,
    value_new,
    key_cache,
    value_cache,
    lengths,
    table,
    gain,
    gate_weight,
    up_weight,
    down_weight,
):
    rows, depth = hidden_in.shape
    blocks = depth // HEAD
    width = lax.axis_size("wide")
    members = width // GROUPS
    chips = members // 2

    def pairs(x):
        return x.reshape(rows, blocks, HEAD).transpose(1, 0, 2).reshape(rows * blocks, HEAD)

    normed, resid = attend(
        rows,
        lengths,
        pairs(hidden_in),
        pairs(queries),
        key_new,
        value_new,
        key_cache,
        value_cache,
        gain.reshape(blocks, HEAD),
    )
    twin = swap(normed, members, width)
    normed, gate_weight = fetch(normed, normed, gate_weight)
    both = jnp.stack([normed, twin], 0)
    came = [swap(both, 2 * k, width) for k in range(1, chips)]
    both, up_weight, down_weight = fetch(both, both, up_weight, down_weight)
    mine = join([both] + came).reshape(members, blocks, rows, HEAD).transpose(0, 2, 1, 3).reshape(members * rows, depth)
    other = swap(mine, 1, width)
    table = table.reshape(1, width)
    units = gate_weight.shape[1]
    size = members * rows * depth * units
    hidden = here(
        functools.partial(hidden_kernel, rows, width, 0),
        (members * rows, units), 2 * size, "feed_own", mine, table, gate_weight, up_weight,
    )
    sent = here(
        functools.partial(feed_kernel, rows, width, members),
        mine.shape, 3 * size, "feed_other", hidden, other, table, gate_weight, up_weight, down_weight,
    )
    came = swap(sent, 1, width)
    kept = here(down_kernel, mine.shape, size, "down_own", sent, hidden, down_weight)
    summed = kept.astype(F32) + came.astype(F32)
    half = chips * rows

    def gather(first):
        total = summed[first : first + rows]
        for k in range(1, chips):
            at = first + k * rows
            total = total + swap(summed[at : at + rows].astype(BF16), 2 * k, width).astype(F32)
        return total

    other = swap(gather(half).astype(BF16), members, width)
    ffn_out = (gather(0) + other.astype(F32)).astype(BF16).astype(F32)
    resid = resid.reshape(blocks, rows, HEAD).transpose(1, 0, 2).reshape(rows, depth)
    return (resid + ffn_out).astype(BF16)


def solution(mesh):
    in_specs = (
        P(("parts", "wide"), None),
        P(("parts", "wide"), None),
        P(("parts", "wide"), None),
        P(("parts", "wide"), None),
        P(("parts", "wide"), None),
        P(("parts", "wide"), None),
        P(("parts", "wide")),
        P("parts", None),
        P(),
        P(None, "wide"),
        P(None, "wide"),
        P("wide", None),
    )
    out_specs = P(("parts", "wide"), None)
    return jax.shard_map(local, mesh=mesh, in_specs=in_specs, out_specs=out_specs, check_vma=False)
```

```python
import functools

import jax
import jax.numpy as jnp
from jax import lax
from jax.experimental import pallas as pl
from jax.experimental.pallas import tpu as pltpu
from jax.sharding import PartitionSpec as P

HEADS = 64
KV_HEADS = 8
HEAD = 128
GROUPS = 2
F32 = jnp.float32
BF16 = jnp.bfloat16
VMEM = pltpu.VMEM
SMEM = pltpu.SMEM


def attend_kernel(rows, len_ref, hid_ref, q_ref, kn_ref, vn_ref, kc_ref, vc_ref, gain_ref, normed_ref, resid_ref, wide_gain):
    total = q_ref.shape[0]
    part = total // KV_HEADS
    cached = kc_ref.shape[0]
    for r in range(rows):
        wide_gain[pl.ds(r, total // rows, stride=rows), :] = gain_ref[...]
    scale = HEAD ** -0.5
    scores = jnp.concatenate(
        [
            lax.dot_general(
                q_ref[k * part : (k + 1) * part, :],
                kc_ref[:, k * HEAD : (k + 1) * HEAD],
                (((1,), (1,)), ((), ())),
                preferred_element_type=F32,
            )
            for k in range(KV_HEADS)
        ],
        0,
    ) * scale
    seen = lax.broadcasted_iota(jnp.int32, (total, cached), 1) < len_ref[0]
    scores = jnp.where(seen, scores, -1e30)
    turn = lax.broadcasted_iota(jnp.int32, (total, 1), 0) % rows
    query = q_ref[...].astype(F32)
    fresh = []
    values = []
    for t in range(rows):
        keys = jnp.concatenate(
            [
                jnp.broadcast_to(kn_ref[t : t + 1, k * HEAD : (k + 1) * HEAD].astype(F32), (part, HEAD))
                for k in range(KV_HEADS)
            ],
            0,
        )
        score = jnp.sum(query * keys, axis=1, keepdims=True) * scale
        fresh.append(jnp.where(turn >= t, score, -1e30))
        values.append(
            jnp.concatenate(
                [
                    jnp.broadcast_to(vn_ref[t : t + 1, k * HEAD : (k + 1) * HEAD].astype(F32), (part, HEAD))
                    for k in range(KV_HEADS)
                ],
                0,
            )
        )
    top = jnp.max(scores, axis=1, keepdims=True)
    for score in fresh:
        top = jnp.maximum(top, score)
    raised = jnp.exp(scores - top)
    bottom = jnp.sum(raised, axis=1, keepdims=True)
    lifted = [jnp.exp(score - top) for score in fresh]
    for value in lifted:
        bottom = bottom + value
    probs = (raised / bottom).astype(BF16)
    context = jnp.concatenate(
        [
            jnp.dot(
                probs[k * part : (k + 1) * part, :],
                vc_ref[:, k * HEAD : (k + 1) * HEAD],
                preferred_element_type=F32,
            )
            for k in range(KV_HEADS)
        ],
        0,
    )
    for value, column in zip(lifted, values):
        context = context + (value / bottom).astype(BF16).astype(F32) * column
    resid = hid_ref[...].astype(F32) + context.astype(BF16).astype(F32)
    resid_ref[...] = resid
    square = jnp.sum(resid * resid, axis=1, keepdims=True)
    factor = jnp.zeros((total, 1), F32)
    width = total // rows * HEAD
    for r in range(rows):
        mean = jnp.sum(jnp.where(turn == r, square, 0.0), axis=0, keepdims=True) / width
        factor = jnp.where(turn == r, lax.rsqrt(mean + 1e-05), factor)
    normed_ref[...] = (resid * factor * wide_gain[...]).astype(BF16)


def attend(rows, lengths, hidden, query, key_new, value_new, key_cache, value_cache, gain):
    vmem = pl.BlockSpec(memory_space=VMEM)
    return pl.pallas_call(
        functools.partial(attend_kernel, rows),
        out_shape=(
            VMEM(hidden.shape, BF16),
            VMEM(hidden.shape, F32),
        ),
        in_specs=[pl.BlockSpec(memory_space=SMEM)] + [vmem] * 7,
        out_specs=(vmem, vmem),
        scratch_shapes=[VMEM(hidden.shape, F32)],
        name="attend",
    )(lengths, hidden, query, key_new, value_new, key_cache, value_cache, gain)


FETCHES = 4


def fetch_kernel(count, after_ref, carry_ref, *refs):
    sources, passed_ref, targets, sems = refs[:count], refs[count], refs[count + 1 : -1], refs[-1]
    copies = []
    for which in range(count):
        size = sources[which].shape[0] // FETCHES
        for i in range(FETCHES):
            span = pl.ds(i * size, size)
            copies.append(
                pltpu.make_async_copy(
                    sources[which].at[span, :], targets[which].at[span, :], sems.at[which * FETCHES + i]
                )
            )
            copies[-1].start()
    passed_ref[...] = carry_ref[...]
    for copy in copies:
        copy.wait()


def fetch(after, carry, *weights):
    vmem = pl.BlockSpec(memory_space=VMEM)
    count = len(weights)
    return pl.pallas_call(
        functools.partial(fetch_kernel, count),
        out_shape=tuple(VMEM(a.shape, a.dtype) for a in (carry, *weights)),
        in_specs=[pl.BlockSpec(memory_space=pl.ANY), vmem] + [pl.BlockSpec(memory_space=pltpu.HBM)] * count,
        out_specs=(vmem,) * (count + 1),
        scratch_shapes=[pltpu.SemaphoreType.DMA((count * FETCHES,))],
        cost_estimate=pl.CostEstimate(
            flops=0, bytes_accessed=sum(4 * w.size for w in weights), transcendentals=0
        ),
        compiler_params=pltpu.CompilerParams(vmem_limit_bytes=4 << 20),
        name="fetch",
    )(after, carry, *[pltpu.with_memory_space_constraint(w, pltpu.HBM) for w in weights])


def join_kernel(*refs):
    for at, ref in enumerate(refs[:-1]):
        refs[-1][:, at] = ref[...]


def join(parts):
    vmem = pl.BlockSpec(memory_space=VMEM)
    return pl.pallas_call(
        join_kernel,
        out_shape=VMEM((parts[0].shape[0], len(parts), *parts[0].shape[1:]), parts[0].dtype),
        in_specs=[vmem] * len(parts),
        out_specs=vmem,
        compiler_params=pltpu.CompilerParams(vmem_limit_bytes=4 << 20),
        name="join",
    )(*parts)


CHUNK = 1024


def hidden_rows(new, width, first, x_ref, table_ref, gate_ref, up_ref):
    rows, depth = x_ref.shape
    units = gate_ref.shape[1]
    gate = jnp.zeros((rows, units), F32)
    upper = jnp.zeros((rows, units), F32)
    for at in range(0, depth, CHUNK):
        block = x_ref[:, at : at + CHUNK]
        gate += jnp.dot(block, gate_ref[at : at + CHUNK, :], preferred_element_type=F32)
        upper += jnp.dot(block, up_ref[at : at + CHUNK, :], preferred_element_type=F32)
    hidden = gate / (1.0 + jnp.exp(-gate)) * upper
    members = width // GROUPS
    chips = members // 2
    me = lax.axis_index("wide")
    block = first + lax.broadcasted_iota(jnp.int32, (rows, width), 0) // new
    group, chip = block % members // chips, block % chips
    source = me ^ (block // members) ^ (group * (members + 1)) ^ (chip * 2 + (chip > 0).astype(jnp.int32))
    column = lax.broadcasted_iota(jnp.int32, (rows, width), 1)
    served = (source == column) & (table_ref[...] == me // members)
    keep = jnp.sum(served.astype(jnp.int32), axis=1, keepdims=True) > 0
    return jnp.where(keep, hidden, 0.0).astype(BF16)


def down_rows(hidden, down_ref, out_ref):
    for at in range(0, out_ref.shape[1], CHUNK):
        out_ref[:, at : at + CHUNK] = jnp.dot(
            hidden, down_ref[:, at : at + CHUNK], preferred_element_type=F32
        ).astype(BF16)


def hidden_kernel(new, width, first, x_ref, table_ref, gate_ref, up_ref, out_ref):
    out_ref[...] = hidden_rows(new, width, first, x_ref, table_ref, gate_ref, up_ref)


def feed_kernel(new, width, first, after_ref, x_ref, table_ref, gate_ref, up_ref, down_ref, out_ref):
    down_rows(hidden_rows(new, width, first, x_ref, table_ref, gate_ref, up_ref), down_ref, out_ref)


def down_kernel(after_ref, hidden_ref, down_ref, out_ref):
    down_rows(hidden_ref[...], down_ref, out_ref)


def here(kernel, out_shape, products, name, *operands):
    vmem = pl.BlockSpec(memory_space=VMEM)
    return pl.pallas_call(
        kernel,
        out_shape=VMEM(out_shape, BF16),
        in_specs=[vmem] * len(operands),
        out_specs=vmem,
        compiler_params=pltpu.CompilerParams(vmem_limit_bytes=16 << 20),
        cost_estimate=pl.CostEstimate(flops=2 * products, bytes_accessed=4 << 20, transcendentals=0),
        name=name,
    )(*[pltpu.with_memory_space_constraint(x, VMEM) for x in operands])


def swap(x, bits, width):
    return lax.ppermute(x, "wide", [(i, i ^ bits) for i in range(width)])


def local(
    hidden_in,
    queries,
    key_new,
    value_new,
    key_cache,
    value_cache,
    lengths,
    table,
    gain,
    gate_weight,
    up_weight,
    down_weight,
):
    rows, depth = hidden_in.shape
    blocks = depth // HEAD
    width = lax.axis_size("wide")
    members = width // GROUPS
    chips = members // 2

    def pairs(x):
        return x.reshape(rows, blocks, HEAD).transpose(1, 0, 2).reshape(rows * blocks, HEAD)

    normed, resid = attend(
        rows,
        lengths,
        pairs(hidden_in),
        pairs(queries),
        key_new,
        value_new,
        key_cache,
        value_cache,
        gain.reshape(blocks, HEAD),
    )
    twin = swap(normed, members + 1, width)
    normed, gate_weight = fetch(normed, normed, gate_weight)
    both = jnp.stack([normed, twin], 0)
    came = [swap(both, 2 * k + 1, width) for k in range(1, chips)]
    both, up_weight, down_weight = fetch(both, both, up_weight, down_weight)
    mine = join([both] + came).reshape(members, blocks, rows, HEAD).transpose(0, 2, 1, 3).reshape(members * rows, depth)
    other = swap(mine, 1, width)
    table = table.reshape(1, width)
    units = gate_weight.shape[1]
    size = members * rows * depth * units
    hidden = here(
        functools.partial(hidden_kernel, rows, width, 0),
        (members * rows, units), 2 * size, "feed_own", mine, table, gate_weight, up_weight,
    )
    sent = here(
        functools.partial(feed_kernel, rows, width, members),
        mine.shape, 3 * size, "feed_other", hidden, other, table, gate_weight, up_weight, down_weight,
    )
    came = swap(sent, 1, width)
    kept = here(down_kernel, mine.shape, size, "down_own", sent, hidden, down_weight)
    summed = kept.astype(F32) + came.astype(F32)
    half = chips * rows

    def gather(first):
        total = summed[first : first + rows]
        for k in range(1, chips):
            at = first + k * rows
            total = total + swap(summed[at : at + rows].astype(BF16), 2 * k + 1, width).astype(F32)
        return total

    other = swap(gather(half).astype(BF16), members + 1, width)
    ffn_out = (gather(0) + other.astype(F32)).astype(BF16).astype(F32)
    resid = resid.reshape(blocks, rows, HEAD).transpose(1, 0, 2).reshape(rows, depth)
    return (resid + ffn_out).astype(BF16)


def solution(mesh):
    in_specs = (
        P(("parts", "wide"), None),
        P(("parts", "wide"), None),
        P(("parts", "wide"), None),
        P(("parts", "wide"), None),
        P(("parts", "wide"), None),
        P(("parts", "wide"), None),
        P(("parts", "wide")),
        P("parts", None),
        P(),
        P(None, "wide"),
        P(None, "wide"),
        P("wide", None),
    )
    out_specs = P(("parts", "wide"), None)
    return jax.shard_map(local, mesh=mesh, in_specs=in_specs, out_specs=out_specs, check_vma=False)
```

```python
import functools

import jax
import jax.numpy as jnp
from jax import lax
from jax.experimental import pallas as pl
from jax.experimental.pallas import tpu as pltpu
from jax.sharding import PartitionSpec as P

HEADS = 64
KV_HEADS = 8
HEAD = 128
GROUPS = 2
F32 = jnp.float32
BF16 = jnp.bfloat16
VMEM = pltpu.VMEM
SMEM = pltpu.SMEM


def first_kernel(out_ref):
    out_ref[...] = jnp.zeros_like(out_ref)


def first():
    return pl.pallas_call(
        first_kernel,
        out_shape=VMEM((8, HEAD), F32),
        out_specs=pl.BlockSpec(memory_space=VMEM),
        cost_estimate=pl.CostEstimate(flops=20_000_000_000, bytes_accessed=0, transcendentals=0),
        compiler_params=pltpu.CompilerParams(vmem_limit_bytes=1 << 20),
        name="first",
    )()


def attend_kernel(rows, after_ref, len_ref, hid_ref, q_ref, kn_ref, vn_ref, kc_ref, vc_ref, gain_ref, normed_ref, resid_ref, wide_gain):
    total = q_ref.shape[0]
    part = total // KV_HEADS
    cached = kc_ref.shape[0]
    for r in range(rows):
        wide_gain[pl.ds(r, total // rows, stride=rows), :] = gain_ref[...]
    scale = HEAD ** -0.5
    scores = jnp.concatenate(
        [
            lax.dot_general(
                q_ref[k * part : (k + 1) * part, :],
                kc_ref[:, k * HEAD : (k + 1) * HEAD],
                (((1,), (1,)), ((), ())),
                preferred_element_type=F32,
            )
            for k in range(KV_HEADS)
        ],
        0,
    ) * scale
    seen = lax.broadcasted_iota(jnp.int32, (total, cached), 1) < len_ref[0]
    scores = jnp.where(seen, scores, -1e30)
    turn = lax.broadcasted_iota(jnp.int32, (total, 1), 0) % rows
    query = q_ref[...].astype(F32)
    fresh = []
    values = []
    for t in range(rows):
        keys = jnp.concatenate(
            [
                jnp.broadcast_to(kn_ref[t : t + 1, k * HEAD : (k + 1) * HEAD].astype(F32), (part, HEAD))
                for k in range(KV_HEADS)
            ],
            0,
        )
        score = jnp.sum(query * keys, axis=1, keepdims=True) * scale
        fresh.append(jnp.where(turn >= t, score, -1e30))
        values.append(
            jnp.concatenate(
                [
                    jnp.broadcast_to(vn_ref[t : t + 1, k * HEAD : (k + 1) * HEAD].astype(F32), (part, HEAD))
                    for k in range(KV_HEADS)
                ],
                0,
            )
        )
    top = jnp.max(scores, axis=1, keepdims=True)
    for score in fresh:
        top = jnp.maximum(top, score)
    raised = jnp.exp(scores - top)
    bottom = jnp.sum(raised, axis=1, keepdims=True)
    lifted = [jnp.exp(score - top) for score in fresh]
    for value in lifted:
        bottom = bottom + value
    probs = (raised / bottom).astype(BF16)
    context = jnp.concatenate(
        [
            jnp.dot(
                probs[k * part : (k + 1) * part, :],
                vc_ref[:, k * HEAD : (k + 1) * HEAD],
                preferred_element_type=F32,
            )
            for k in range(KV_HEADS)
        ],
        0,
    )
    for value, column in zip(lifted, values):
        context = context + (value / bottom).astype(BF16).astype(F32) * column
    resid = hid_ref[...].astype(F32) + context.astype(BF16).astype(F32)
    resid_ref[...] = resid
    square = jnp.sum(resid * resid, axis=1, keepdims=True)
    factor = jnp.zeros((total, 1), F32)
    width = total // rows * HEAD
    for r in range(rows):
        mean = jnp.sum(jnp.where(turn == r, square, 0.0), axis=0, keepdims=True) / width
        factor = jnp.where(turn == r, lax.rsqrt(mean + 1e-05), factor)
    normed_ref[...] = (resid * factor * wide_gain[...]).astype(BF16)


def attend(rows, lengths, hidden, query, key_new, value_new, key_cache, value_cache, gain):
    vmem = pl.BlockSpec(memory_space=VMEM)
    return pl.pallas_call(
        functools.partial(attend_kernel, rows),
        out_shape=(
            VMEM(hidden.shape, BF16),
            VMEM(hidden.shape, F32),
        ),
        in_specs=[vmem, pl.BlockSpec(memory_space=SMEM)] + [vmem] * 7,
        out_specs=(vmem, vmem),
        scratch_shapes=[VMEM(hidden.shape, F32)],
        compiler_params=pltpu.CompilerParams(vmem_limit_bytes=8 << 20),
        name="attend",
    )(first(), lengths, hidden, query, key_new, value_new, key_cache, value_cache, gain)


FETCHES = 4


def fetch_kernel(count, after_ref, carry_ref, *refs):
    sources, passed_ref, targets, sems = refs[:count], refs[count], refs[count + 1 : -1], refs[-1]
    copies = []
    for which in range(count):
        size = sources[which].shape[0] // FETCHES
        for i in range(FETCHES):
            span = pl.ds(i * size, size)
            copies.append(
                pltpu.make_async_copy(
                    sources[which].at[span, :], targets[which].at[span, :], sems.at[which * FETCHES + i]
                )
            )
            copies[-1].start()
    passed_ref[...] = carry_ref[...]
    for copy in copies:
        copy.wait()


def fetch(after, carry, *weights):
    vmem = pl.BlockSpec(memory_space=VMEM)
    count = len(weights)
    return pl.pallas_call(
        functools.partial(fetch_kernel, count),
        out_shape=tuple(VMEM(a.shape, a.dtype) for a in (carry, *weights)),
        in_specs=[pl.BlockSpec(memory_space=pl.ANY), vmem] + [pl.BlockSpec(memory_space=pltpu.HBM)] * count,
        out_specs=(vmem,) * (count + 1),
        scratch_shapes=[pltpu.SemaphoreType.DMA((count * FETCHES,))],
        cost_estimate=pl.CostEstimate(
            flops=0, bytes_accessed=sum(4 * w.size for w in weights), transcendentals=0
        ),
        compiler_params=pltpu.CompilerParams(vmem_limit_bytes=4 << 20),
        name="fetch",
    )(after, carry, *[pltpu.with_memory_space_constraint(w, pltpu.HBM) for w in weights])


def join_kernel(*refs):
    for at, ref in enumerate(refs[:-1]):
        refs[-1][:, at] = ref[...]


def join(parts):
    vmem = pl.BlockSpec(memory_space=VMEM)
    return pl.pallas_call(
        join_kernel,
        out_shape=VMEM((parts[0].shape[0], len(parts), *parts[0].shape[1:]), parts[0].dtype),
        in_specs=[vmem] * len(parts),
        out_specs=vmem,
        compiler_params=pltpu.CompilerParams(vmem_limit_bytes=4 << 20),
        name="join",
    )(*parts)


CHUNK = 1024


def hidden_rows(new, width, first, x_ref, table_ref, gate_ref, up_ref):
    rows, depth = x_ref.shape
    units = gate_ref.shape[1]
    gate = jnp.zeros((rows, units), F32)
    upper = jnp.zeros((rows, units), F32)
    for at in range(0, depth, CHUNK):
        block = x_ref[:, at : at + CHUNK]
        gate += jnp.dot(block, gate_ref[at : at + CHUNK, :], preferred_element_type=F32)
        upper += jnp.dot(block, up_ref[at : at + CHUNK, :], preferred_element_type=F32)
    hidden = gate / (1.0 + jnp.exp(-gate)) * upper
    members = width // GROUPS
    chips = members // 2
    me = lax.axis_index("wide")
    block = first + lax.broadcasted_iota(jnp.int32, (rows, width), 0) // new
    group, chip = block % members // chips, block % chips
    source = me ^ (block // members) ^ (group * (members + 1)) ^ (chip * 2 + (chip > 0).astype(jnp.int32))
    column = lax.broadcasted_iota(jnp.int32, (rows, width), 1)
    served = (source == column) & (table_ref[...] == me // members)
    keep = jnp.sum(served.astype(jnp.int32), axis=1, keepdims=True) > 0
    return jnp.where(keep, hidden, 0.0).astype(BF16)


def down_rows(hidden, down_ref, out_ref):
    for at in range(0, out_ref.shape[1], CHUNK):
        out_ref[:, at : at + CHUNK] = jnp.dot(
            hidden, down_ref[:, at : at + CHUNK], preferred_element_type=F32
        ).astype(BF16)


def hidden_kernel(new, width, first, x_ref, table_ref, gate_ref, up_ref, out_ref):
    out_ref[...] = hidden_rows(new, width, first, x_ref, table_ref, gate_ref, up_ref)


def feed_kernel(new, width, first, after_ref, x_ref, table_ref, gate_ref, up_ref, down_ref, out_ref):
    down_rows(hidden_rows(new, width, first, x_ref, table_ref, gate_ref, up_ref), down_ref, out_ref)


def down_kernel(after_ref, hidden_ref, down_ref, out_ref):
    down_rows(hidden_ref[...], down_ref, out_ref)


def here(kernel, out_shape, products, name, *operands):
    vmem = pl.BlockSpec(memory_space=VMEM)
    return pl.pallas_call(
        kernel,
        out_shape=VMEM(out_shape, BF16),
        in_specs=[vmem] * len(operands),
        out_specs=vmem,
        compiler_params=pltpu.CompilerParams(vmem_limit_bytes=16 << 20),
        cost_estimate=pl.CostEstimate(flops=2 * products, bytes_accessed=4 << 20, transcendentals=0),
        name=name,
    )(*[pltpu.with_memory_space_constraint(x, VMEM) for x in operands])


def swap(x, bits, width):
    return lax.ppermute(x, "wide", [(i, i ^ bits) for i in range(width)])


def local(
    hidden_in,
    queries,
    key_new,
    value_new,
    key_cache,
    value_cache,
    lengths,
    table,
    gain,
    gate_weight,
    up_weight,
    down_weight,
):
    rows, depth = hidden_in.shape
    blocks = depth // HEAD
    width = lax.axis_size("wide")
    members = width // GROUPS
    chips = members // 2

    def pairs(x):
        return x.reshape(rows, blocks, HEAD).transpose(1, 0, 2).reshape(rows * blocks, HEAD)

    normed, resid = attend(
        rows,
        lengths,
        pairs(hidden_in),
        pairs(queries),
        key_new,
        value_new,
        key_cache,
        value_cache,
        gain.reshape(blocks, HEAD),
    )
    twin = swap(normed, members + 1, width)
    normed, gate_weight = fetch(normed, normed, gate_weight)
    both = jnp.stack([normed, twin], 0)
    came = [swap(both, 2 * k + 1, width) for k in range(1, chips)]
    both, up_weight, down_weight = fetch(both, both, up_weight, down_weight)
    mine = join([both] + came).reshape(members, blocks, rows, HEAD).transpose(0, 2, 1, 3).reshape(members * rows, depth)
    other = swap(mine, 1, width)
    table = table.reshape(1, width)
    units = gate_weight.shape[1]
    size = members * rows * depth * units
    hidden = here(
        functools.partial(hidden_kernel, rows, width, 0),
        (members * rows, units), 2 * size, "feed_own", mine, table, gate_weight, up_weight,
    )
    sent = here(
        functools.partial(feed_kernel, rows, width, members),
        mine.shape, 3 * size, "feed_other", hidden, other, table, gate_weight, up_weight, down_weight,
    )
    came = swap(sent, 1, width)
    kept = here(down_kernel, mine.shape, size, "down_own", sent, hidden, down_weight)
    summed = kept.astype(F32) + came.astype(F32)
    half = chips * rows

    def gather(first):
        total = summed[first : first + rows]
        for k in range(1, chips):
            at = first + k * rows
            total = total + swap(summed[at : at + rows].astype(BF16), 2 * k + 1, width).astype(F32)
        return total

    other = swap(gather(half).astype(BF16), members + 1, width)
    ffn_out = (gather(0) + other.astype(F32)).astype(BF16).astype(F32)
    resid = resid.reshape(blocks, rows, HEAD).transpose(1, 0, 2).reshape(rows, depth)
    return (resid + ffn_out).astype(BF16)


def solution(mesh):
    in_specs = (
        P(("parts", "wide"), None),
        P(("parts", "wide"), None),
        P(("parts", "wide"), None),
        P(("parts", "wide"), None),
        P(("parts", "wide"), None),
        P(("parts", "wide"), None),
        P(("parts", "wide")),
        P("parts", None),
        P(),
        P(None, "wide"),
        P(None, "wide"),
        P("wide", None),
    )
    out_specs = P(("parts", "wide"), None)
    return jax.shard_map(local, mesh=mesh, in_specs=in_specs, out_specs=out_specs, check_vma=False)
```

```python
import functools

import jax
import jax.numpy as jnp
from jax import lax
from jax.experimental import pallas as pl
from jax.experimental.pallas import tpu as pltpu
from jax.sharding import PartitionSpec as P

HEADS = 64
KV_HEADS = 8
HEAD = 128
GROUPS = 2
F32 = jnp.float32
BF16 = jnp.bfloat16
VMEM = pltpu.VMEM
SMEM = pltpu.SMEM


def first_kernel(out_ref):
    out_ref[...] = jnp.zeros_like(out_ref)


def first():
    return pl.pallas_call(
        first_kernel,
        out_shape=VMEM((8, HEAD), F32),
        out_specs=pl.BlockSpec(memory_space=VMEM),
        cost_estimate=pl.CostEstimate(flops=20_000_000_000, bytes_accessed=0, transcendentals=0),
        compiler_params=pltpu.CompilerParams(vmem_limit_bytes=1 << 20),
        name="first",
    )()


def attend_kernel(rows, after_ref, len_ref, hid_ref, q_ref, kn_ref, vn_ref, kc_ref, vc_ref, gain_ref, normed_ref, resid_ref, wide_gain):
    total = q_ref.shape[0]
    part = total // KV_HEADS
    cached = kc_ref.shape[0]
    for r in range(rows):
        wide_gain[pl.ds(r, total // rows, stride=rows), :] = gain_ref[...]
    scale = HEAD ** -0.5
    scores = jnp.concatenate(
        [
            lax.dot_general(
                q_ref[k * part : (k + 1) * part, :],
                kc_ref[:, k * HEAD : (k + 1) * HEAD],
                (((1,), (1,)), ((), ())),
                preferred_element_type=F32,
            )
            for k in range(KV_HEADS)
        ],
        0,
    ) * scale
    seen = lax.broadcasted_iota(jnp.int32, (total, cached), 1) < len_ref[0]
    scores = jnp.where(seen, scores, -1e30)
    turn = lax.broadcasted_iota(jnp.int32, (total, 1), 0) % rows
    query = q_ref[...].astype(F32)
    fresh = []
    values = []
    for t in range(rows):
        keys = jnp.concatenate(
            [
                jnp.broadcast_to(kn_ref[t : t + 1, k * HEAD : (k + 1) * HEAD].astype(F32), (part, HEAD))
                for k in range(KV_HEADS)
            ],
            0,
        )
        score = jnp.sum(query * keys, axis=1, keepdims=True) * scale
        fresh.append(jnp.where(turn >= t, score, -1e30))
        values.append(
            jnp.concatenate(
                [
                    jnp.broadcast_to(vn_ref[t : t + 1, k * HEAD : (k + 1) * HEAD].astype(F32), (part, HEAD))
                    for k in range(KV_HEADS)
                ],
                0,
            )
        )
    top = jnp.max(scores, axis=1, keepdims=True)
    for score in fresh:
        top = jnp.maximum(top, score)
    raised = jnp.exp(scores - top)
    bottom = jnp.sum(raised, axis=1, keepdims=True)
    lifted = [jnp.exp(score - top) for score in fresh]
    for value in lifted:
        bottom = bottom + value
    probs = (raised / bottom).astype(BF16)
    context = jnp.concatenate(
        [
            jnp.dot(
                probs[k * part : (k + 1) * part, :],
                vc_ref[:, k * HEAD : (k + 1) * HEAD],
                preferred_element_type=F32,
            )
            for k in range(KV_HEADS)
        ],
        0,
    )
    for value, column in zip(lifted, values):
        context = context + (value / bottom).astype(BF16).astype(F32) * column
    resid = hid_ref[...].astype(F32) + context.astype(BF16).astype(F32)
    resid_ref[...] = resid
    square = jnp.sum(resid * resid, axis=1, keepdims=True)
    factor = jnp.zeros((total, 1), F32)
    width = total // rows * HEAD
    for r in range(rows):
        mean = jnp.sum(jnp.where(turn == r, square, 0.0), axis=0, keepdims=True) / width
        factor = jnp.where(turn == r, lax.rsqrt(mean + 1e-05), factor)
    normed_ref[...] = (resid * factor * wide_gain[...]).astype(BF16)


def attend(rows, lengths, hidden, query, key_new, value_new, key_cache, value_cache, gain):
    vmem = pl.BlockSpec(memory_space=VMEM)
    return pl.pallas_call(
        functools.partial(attend_kernel, rows),
        out_shape=(
            VMEM(hidden.shape, BF16),
            VMEM(hidden.shape, F32),
        ),
        in_specs=[vmem, pl.BlockSpec(memory_space=SMEM)] + [vmem] * 7,
        out_specs=(vmem, vmem),
        scratch_shapes=[VMEM(hidden.shape, F32)],
        compiler_params=pltpu.CompilerParams(vmem_limit_bytes=8 << 20),
        name="attend",
    )(first(), lengths, hidden, query, key_new, value_new, key_cache, value_cache, gain)


FETCHES = 4


def fetch_kernel(count, after_ref, carry_ref, *refs):
    sources, passed_ref, targets, sems = refs[:count], refs[count], refs[count + 1 : -1], refs[-1]
    copies = []
    for which in range(count):
        size = sources[which].shape[0] // FETCHES
        for i in range(FETCHES):
            span = pl.ds(i * size, size)
            copies.append(
                pltpu.make_async_copy(
                    sources[which].at[span, :], targets[which].at[span, :], sems.at[which * FETCHES + i]
                )
            )
            copies[-1].start()
    passed_ref[...] = carry_ref[...]
    for copy in copies:
        copy.wait()


def fetch(after, carry, *weights):
    vmem = pl.BlockSpec(memory_space=VMEM)
    count = len(weights)
    return pl.pallas_call(
        functools.partial(fetch_kernel, count),
        out_shape=tuple(VMEM(a.shape, a.dtype) for a in (carry, *weights)),
        in_specs=[pl.BlockSpec(memory_space=pl.ANY), vmem] + [pl.BlockSpec(memory_space=pltpu.HBM)] * count,
        out_specs=(vmem,) * (count + 1),
        scratch_shapes=[pltpu.SemaphoreType.DMA((count * FETCHES,))],
        cost_estimate=pl.CostEstimate(
            flops=0, bytes_accessed=sum(4 * w.size for w in weights), transcendentals=0
        ),
        compiler_params=pltpu.CompilerParams(vmem_limit_bytes=4 << 20),
        name="fetch",
    )(after, carry, *[pltpu.with_memory_space_constraint(w, pltpu.HBM) for w in weights])


def join_kernel(*refs):
    for at, ref in enumerate(refs[:-1]):
        refs[-1][:, at] = ref[...]


def join(parts):
    vmem = pl.BlockSpec(memory_space=VMEM)
    return pl.pallas_call(
        join_kernel,
        out_shape=VMEM((parts[0].shape[0], len(parts), *parts[0].shape[1:]), parts[0].dtype),
        in_specs=[vmem] * len(parts),
        out_specs=vmem,
        compiler_params=pltpu.CompilerParams(vmem_limit_bytes=4 << 20),
        name="join",
    )(*parts)


CHUNK = 1024


def hidden_rows(new, width, first, x_ref, table_ref, gate_ref, up_ref):
    rows, depth = x_ref.shape
    units = gate_ref.shape[1]
    gate = jnp.zeros((rows, units), F32)
    upper = jnp.zeros((rows, units), F32)
    for at in range(0, depth, CHUNK):
        block = x_ref[:, at : at + CHUNK]
        gate += jnp.dot(block, gate_ref[at : at + CHUNK, :], preferred_element_type=F32)
        upper += jnp.dot(block, up_ref[at : at + CHUNK, :], preferred_element_type=F32)
    hidden = gate / (1.0 + jnp.exp(-gate)) * upper
    members = width // GROUPS
    chips = members // 2
    me = lax.axis_index("wide")
    block = first + lax.broadcasted_iota(jnp.int32, (rows, width), 0) // new
    group, chip = block % members // chips, block % chips
    source = me ^ (block // members) ^ (group * (members + 1)) ^ (chip * 2 + (chip > 0).astype(jnp.int32))
    column = lax.broadcasted_iota(jnp.int32, (rows, width), 1)
    served = (source == column) & (table_ref[...] == me // members)
    keep = jnp.sum(served.astype(jnp.int32), axis=1, keepdims=True) > 0
    return jnp.where(keep, hidden, 0.0).astype(BF16)


def down_rows(hidden, down_ref, out_ref):
    for at in range(0, out_ref.shape[1], CHUNK):
        out_ref[:, at : at + CHUNK] = jnp.dot(
            hidden, down_ref[:, at : at + CHUNK], preferred_element_type=F32
        ).astype(BF16)


def hidden_kernel(new, width, first, x_ref, table_ref, gate_ref, up_ref, out_ref):
    out_ref[...] = hidden_rows(new, width, first, x_ref, table_ref, gate_ref, up_ref)


def feed_kernel(new, width, first, after_ref, x_ref, table_ref, gate_ref, up_ref, down_ref, out_ref):
    down_rows(hidden_rows(new, width, first, x_ref, table_ref, gate_ref, up_ref), down_ref, out_ref)


def down_kernel(after_ref, hidden_ref, down_ref, out_ref):
    down_rows(hidden_ref[...], down_ref, out_ref)


def here(kernel, out_shape, products, name, *operands):
    vmem = pl.BlockSpec(memory_space=VMEM)
    return pl.pallas_call(
        kernel,
        out_shape=VMEM(out_shape, BF16),
        in_specs=[vmem] * len(operands),
        out_specs=vmem,
        compiler_params=pltpu.CompilerParams(vmem_limit_bytes=16 << 20),
        cost_estimate=pl.CostEstimate(flops=2 * products, bytes_accessed=4 << 20, transcendentals=0),
        name=name,
    )(*[pltpu.with_memory_space_constraint(x, VMEM) for x in operands])


def swap(x, bits, width):
    return lax.ppermute(x, "wide", [(i, i ^ bits) for i in range(width)])


def local(
    hidden_in,
    queries,
    key_new,
    value_new,
    key_cache,
    value_cache,
    lengths,
    table,
    gain,
    gate_weight,
    up_weight,
    down_weight,
):
    rows, depth = hidden_in.shape
    blocks = depth // HEAD
    width = lax.axis_size("wide")
    members = width // GROUPS
    chips = members // 2

    def pairs(x):
        return x.reshape(rows, blocks, HEAD).transpose(1, 0, 2).reshape(rows * blocks, HEAD)

    normed, resid = attend(
        rows,
        lengths,
        pairs(hidden_in),
        pairs(queries),
        key_new,
        value_new,
        key_cache,
        value_cache,
        gain.reshape(blocks, HEAD),
    )
    twin = swap(normed, members + 1, width)
    normed, gate_weight = fetch(normed, normed, gate_weight)
    both = jnp.stack([normed, twin], 0)
    came = [swap(both, 2 * k + 1, width) for k in range(1, chips)]
    both, up_weight, down_weight = fetch(both, both, up_weight, down_weight)
    mine = join([both] + came).reshape(members, blocks, rows, HEAD).transpose(0, 2, 1, 3).reshape(members * rows, depth)
    other = swap(mine, 1, width)
    table = table.reshape(1, width)
    units = gate_weight.shape[1]
    size = members * rows * depth * units
    hidden = here(
        functools.partial(hidden_kernel, rows, width, 0),
        (members * rows, units), 2 * size, "feed_own", mine, table, gate_weight, up_weight,
    )
    sent = here(
        functools.partial(feed_kernel, rows, width, members),
        mine.shape, 3 * size, "feed_other", hidden, other, table, gate_weight, up_weight, down_weight,
    )
    came = swap(sent, 1, width)
    kept = here(down_kernel, mine.shape, size, "down_own", sent, hidden, down_weight)
    summed = kept.astype(F32) + came.astype(F32)
    half = chips * rows

    forward = list(range(1, chips))

    def gather(first, order):
        total = summed[first : first + rows]
        for k in order:
            at = first + k * rows
            total = total + swap(summed[at : at + rows].astype(BF16), 2 * k + 1, width).astype(F32)
        return total

    other = swap(gather(half, forward).astype(BF16), members + 1, width)
    ffn_out = (gather(0, forward[::-1]) + other.astype(F32)).astype(BF16).astype(F32)
    resid = resid.reshape(blocks, rows, HEAD).transpose(1, 0, 2).reshape(rows, depth)
    return (resid + ffn_out).astype(BF16)


def solution(mesh):
    in_specs = (
        P(("parts", "wide"), None),
        P(("parts", "wide"), None),
        P(("parts", "wide"), None),
        P(("parts", "wide"), None),
        P(("parts", "wide"), None),
        P(("parts", "wide"), None),
        P(("parts", "wide")),
        P("parts", None),
        P(),
        P(None, "wide"),
        P(None, "wide"),
        P("wide", None),
    )
    out_specs = P(("parts", "wide"), None)
    return jax.shard_map(local, mesh=mesh, in_specs=in_specs, out_specs=out_specs, check_vma=False)
```

```python
import functools

import jax
import jax.numpy as jnp
from jax import lax
from jax.experimental import pallas as pl
from jax.experimental.pallas import tpu as pltpu
from jax.sharding import PartitionSpec as P

HEADS = 64
KV_HEADS = 8
HEAD = 128
GROUPS = 2
F32 = jnp.float32
BF16 = jnp.bfloat16
VMEM = pltpu.VMEM
SMEM = pltpu.SMEM


def first_kernel(out_ref):
    out_ref[...] = jnp.zeros_like(out_ref)


def first():
    return pl.pallas_call(
        first_kernel,
        out_shape=VMEM((8, HEAD), F32),
        out_specs=pl.BlockSpec(memory_space=VMEM),
        cost_estimate=pl.CostEstimate(flops=20_000_000_000, bytes_accessed=0, transcendentals=0),
        compiler_params=pltpu.CompilerParams(vmem_limit_bytes=1 << 20),
        name="first",
    )()


def attend_kernel(rows, after_ref, len_ref, hid_ref, q_ref, kn_ref, vn_ref, kc_ref, vc_ref, gain_ref, normed_ref, resid_ref, wide_gain):
    total = q_ref.shape[0]
    part = total // KV_HEADS
    cached = kc_ref.shape[0]
    for r in range(rows):
        wide_gain[pl.ds(r, total // rows, stride=rows), :] = gain_ref[...]
    scale = HEAD ** -0.5
    scores = jnp.concatenate(
        [
            lax.dot_general(
                q_ref[k * part : (k + 1) * part, :],
                kc_ref[:, k * HEAD : (k + 1) * HEAD],
                (((1,), (1,)), ((), ())),
                preferred_element_type=F32,
            )
            for k in range(KV_HEADS)
        ],
        0,
    ) * scale
    seen = lax.broadcasted_iota(jnp.int32, (total, cached), 1) < len_ref[0]
    scores = jnp.where(seen, scores, -1e30)
    turn = lax.broadcasted_iota(jnp.int32, (total, 1), 0) % rows
    query = q_ref[...].astype(F32)
    fresh = []
    values = []
    for t in range(rows):
        keys = jnp.concatenate(
            [
                jnp.broadcast_to(kn_ref[t : t + 1, k * HEAD : (k + 1) * HEAD].astype(F32), (part, HEAD))
                for k in range(KV_HEADS)
            ],
            0,
        )
        score = jnp.sum(query * keys, axis=1, keepdims=True) * scale
        fresh.append(jnp.where(turn >= t, score, -1e30))
        values.append(
            jnp.concatenate(
                [
                    jnp.broadcast_to(vn_ref[t : t + 1, k * HEAD : (k + 1) * HEAD].astype(F32), (part, HEAD))
                    for k in range(KV_HEADS)
                ],
                0,
            )
        )
    top = jnp.max(scores, axis=1, keepdims=True)
    for score in fresh:
        top = jnp.maximum(top, score)
    raised = jnp.exp(scores - top)
    bottom = jnp.sum(raised, axis=1, keepdims=True)
    lifted = [jnp.exp(score - top) for score in fresh]
    for value in lifted:
        bottom = bottom + value
    probs = (raised / bottom).astype(BF16)
    context = jnp.concatenate(
        [
            jnp.dot(
                probs[k * part : (k + 1) * part, :],
                vc_ref[:, k * HEAD : (k + 1) * HEAD],
                preferred_element_type=F32,
            )
            for k in range(KV_HEADS)
        ],
        0,
    )
    for value, column in zip(lifted, values):
        context = context + (value / bottom).astype(BF16).astype(F32) * column
    resid = hid_ref[...].astype(F32) + context.astype(BF16).astype(F32)
    resid_ref[...] = resid
    square = jnp.sum(resid * resid, axis=1, keepdims=True)
    factor = jnp.zeros((total, 1), F32)
    width = total // rows * HEAD
    for r in range(rows):
        mean = jnp.sum(jnp.where(turn == r, square, 0.0), axis=0, keepdims=True) / width
        factor = jnp.where(turn == r, lax.rsqrt(mean + 1e-05), factor)
    normed_ref[...] = (resid * factor * wide_gain[...]).astype(BF16)


def attend(rows, lengths, hidden, query, key_new, value_new, key_cache, value_cache, gain):
    vmem = pl.BlockSpec(memory_space=VMEM)
    return pl.pallas_call(
        functools.partial(attend_kernel, rows),
        out_shape=(
            VMEM(hidden.shape, BF16),
            VMEM(hidden.shape, F32),
        ),
        in_specs=[vmem, pl.BlockSpec(memory_space=SMEM)] + [vmem] * 7,
        out_specs=(vmem, vmem),
        scratch_shapes=[VMEM(hidden.shape, F32)],
        compiler_params=pltpu.CompilerParams(vmem_limit_bytes=8 << 20),
        name="attend",
    )(first(), lengths, hidden, query, key_new, value_new, key_cache, value_cache, gain)


FETCHES = 4


def fetch_kernel(count, after_ref, carry_ref, *refs):
    sources, passed_ref, targets, sems = refs[:count], refs[count], refs[count + 1 : -1], refs[-1]
    copies = []
    for which in range(count):
        size = sources[which].shape[0] // FETCHES
        for i in range(FETCHES):
            span = pl.ds(i * size, size)
            copies.append(
                pltpu.make_async_copy(
                    sources[which].at[span, :], targets[which].at[span, :], sems.at[which * FETCHES + i]
                )
            )
            copies[-1].start()
    passed_ref[...] = carry_ref[...]
    for copy in copies:
        copy.wait()


def fetch(after, carry, *weights):
    vmem = pl.BlockSpec(memory_space=VMEM)
    count = len(weights)
    return pl.pallas_call(
        functools.partial(fetch_kernel, count),
        out_shape=tuple(VMEM(a.shape, a.dtype) for a in (carry, *weights)),
        in_specs=[pl.BlockSpec(memory_space=pl.ANY), vmem] + [pl.BlockSpec(memory_space=pltpu.HBM)] * count,
        out_specs=(vmem,) * (count + 1),
        scratch_shapes=[pltpu.SemaphoreType.DMA((count * FETCHES,))],
        cost_estimate=pl.CostEstimate(
            flops=0, bytes_accessed=sum(4 * w.size for w in weights), transcendentals=0
        ),
        compiler_params=pltpu.CompilerParams(vmem_limit_bytes=4 << 20),
        name="fetch",
    )(after, carry, *[pltpu.with_memory_space_constraint(w, pltpu.HBM) for w in weights])


def join_kernel(*refs):
    for at, ref in enumerate(refs[:-1]):
        refs[-1][:, at] = ref[...]


def join(parts):
    vmem = pl.BlockSpec(memory_space=VMEM)
    return pl.pallas_call(
        join_kernel,
        out_shape=VMEM((parts[0].shape[0], len(parts), *parts[0].shape[1:]), parts[0].dtype),
        in_specs=[vmem] * len(parts),
        out_specs=vmem,
        compiler_params=pltpu.CompilerParams(vmem_limit_bytes=4 << 20),
        name="join",
    )(*parts)


CHUNK = 1024


def hidden_rows(new, width, first, x_ref, table_ref, gate_ref, up_ref):
    rows, depth = x_ref.shape
    units = gate_ref.shape[1]
    gate = jnp.zeros((rows, units), F32)
    upper = jnp.zeros((rows, units), F32)
    for at in range(0, depth, CHUNK):
        block = x_ref[:, at : at + CHUNK]
        gate += jnp.dot(block, gate_ref[at : at + CHUNK, :], preferred_element_type=F32)
        upper += jnp.dot(block, up_ref[at : at + CHUNK, :], preferred_element_type=F32)
    hidden = gate / (1.0 + jnp.exp(-gate)) * upper
    members = width // GROUPS
    chips = members // 2
    me = lax.axis_index("wide")
    block = first + lax.broadcasted_iota(jnp.int32, (rows, width), 0) // new
    group, chip = block % members // chips, block % chips
    source = me ^ (block // members) ^ (group * (members + 1)) ^ (chip * 2 + (chip > 0).astype(jnp.int32))
    column = lax.broadcasted_iota(jnp.int32, (rows, width), 1)
    served = (source == column) & (table_ref[...] == me // members)
    keep = jnp.sum(served.astype(jnp.int32), axis=1, keepdims=True) > 0
    return jnp.where(keep, hidden, 0.0).astype(BF16)


def down_rows(hidden, down_ref, own_ref, twin_ref):
    half, depth = own_ref.shape
    for at in range(0, depth, CHUNK):
        out = jnp.dot(hidden, down_ref[:, at : at + CHUNK], preferred_element_type=F32)
        own_ref[:, at : at + CHUNK] = out[:half].astype(BF16)
        twin_ref[:, at : at + CHUNK] = out[half:].astype(BF16)


def hidden_kernel(new, width, first, x_ref, table_ref, gate_ref, up_ref, out_ref):
    out_ref[...] = hidden_rows(new, width, first, x_ref, table_ref, gate_ref, up_ref)


def feed_kernel(new, width, first, after_ref, x_ref, table_ref, gate_ref, up_ref, down_ref, own_ref, twin_ref):
    hidden = hidden_rows(new, width, first, x_ref, table_ref, gate_ref, up_ref)
    down_rows(hidden, down_ref, own_ref, twin_ref)


def down_kernel(after_ref, hidden_ref, down_ref, own_ref, twin_ref):
    down_rows(hidden_ref[...], down_ref, own_ref, twin_ref)


def here(kernel, out_shapes, products, name, *operands):
    vmem = pl.BlockSpec(memory_space=VMEM)
    return pl.pallas_call(
        kernel,
        out_shape=tuple(VMEM(shape, BF16) for shape in out_shapes),
        in_specs=[vmem] * len(operands),
        out_specs=(vmem,) * len(out_shapes),
        compiler_params=pltpu.CompilerParams(vmem_limit_bytes=16 << 20),
        cost_estimate=pl.CostEstimate(flops=2 * products, bytes_accessed=4 << 20, transcendentals=0),
        name=name,
    )(*[pltpu.with_memory_space_constraint(x, VMEM) for x in operands])


def swap(x, bits, width):
    return lax.ppermute(x, "wide", [(i, i ^ bits) for i in range(width)])


def local(
    hidden_in,
    queries,
    key_new,
    value_new,
    key_cache,
    value_cache,
    lengths,
    table,
    gain,
    gate_weight,
    up_weight,
    down_weight,
):
    rows, depth = hidden_in.shape
    blocks = depth // HEAD
    width = lax.axis_size("wide")
    members = width // GROUPS
    chips = members // 2

    def pairs(x):
        return x.reshape(rows, blocks, HEAD).transpose(1, 0, 2).reshape(rows * blocks, HEAD)

    normed, resid = attend(
        rows,
        lengths,
        pairs(hidden_in),
        pairs(queries),
        key_new,
        value_new,
        key_cache,
        value_cache,
        gain.reshape(blocks, HEAD),
    )
    twin = swap(normed, members + 1, width)
    normed, gate_weight = fetch(normed, normed, gate_weight)
    both = jnp.stack([normed, twin], 0)
    came = [swap(both, 2 * k + 1, width) for k in range(1, chips)]
    both, up_weight, down_weight = fetch(both, both, up_weight, down_weight)
    mine = join([both] + came).reshape(members, blocks, rows, HEAD).transpose(0, 2, 1, 3).reshape(members * rows, depth)
    other = swap(mine, 1, width)
    table = table.reshape(1, width)
    units = gate_weight.shape[1]
    size = members * rows * depth * units
    (hidden,) = here(
        functools.partial(hidden_kernel, rows, width, 0),
        [(members * rows, units)], 2 * size, "feed_own", mine, table, gate_weight, up_weight,
    )
    halves = [(chips * rows, depth)] * 2
    sent_own, sent_twin = here(
        functools.partial(feed_kernel, rows, width, members),
        halves, 3 * size, "feed_other", hidden, other, table, gate_weight, up_weight, down_weight,
    )
    came_twin = swap(sent_twin, 1, width)
    came_own = swap(sent_own, 1, width)
    kept_own, kept_twin = here(down_kernel, halves, size, "down_own", sent_twin, hidden, down_weight)

    forward = list(range(1, chips))

    def gather(kept, came, order):
        summed = kept.astype(F32) + came.astype(F32)
        total = summed[:rows]
        for k in order:
            at = k * rows
            total = total + swap(summed[at : at + rows].astype(BF16), 2 * k + 1, width).astype(F32)
        return total

    other = swap(gather(kept_twin, came_twin, forward[-1:] + forward[:-1]).astype(BF16), members + 1, width)
    ffn_out = (gather(kept_own, came_own, forward[::-1]) + other.astype(F32)).astype(BF16).astype(F32)
    resid = resid.reshape(blocks, rows, HEAD).transpose(1, 0, 2).reshape(rows, depth)
    return (resid + ffn_out).astype(BF16)


def solution(mesh):
    in_specs = (
        P(("parts", "wide"), None),
        P(("parts", "wide"), None),
        P(("parts", "wide"), None),
        P(("parts", "wide"), None),
        P(("parts", "wide"), None),
        P(("parts", "wide"), None),
        P(("parts", "wide")),
        P("parts", None),
        P(),
        P(None, "wide"),
        P(None, "wide"),
        P("wide", None),
    )
    out_specs = P(("parts", "wide"), None)
    return jax.shard_map(local, mesh=mesh, in_specs=in_specs, out_specs=out_specs, check_vma=False)
```

```python
import functools

import jax
import jax.numpy as jnp
from jax import lax
from jax.experimental import pallas as pl
from jax.experimental.pallas import tpu as pltpu
from jax.sharding import PartitionSpec as P

HEADS = 64
KV_HEADS = 8
HEAD = 128
GROUPS = 2
F32 = jnp.float32
BF16 = jnp.bfloat16
VMEM = pltpu.VMEM
SMEM = pltpu.SMEM


def first_kernel(out_ref):
    out_ref[...] = jnp.zeros_like(out_ref)


def first():
    return pl.pallas_call(
        first_kernel,
        out_shape=VMEM((8, HEAD), F32),
        out_specs=pl.BlockSpec(memory_space=VMEM),
        cost_estimate=pl.CostEstimate(flops=20_000_000_000, bytes_accessed=0, transcendentals=0),
        compiler_params=pltpu.CompilerParams(vmem_limit_bytes=1 << 20),
        name="first",
    )()


def attend_kernel(rows, after_ref, len_ref, hid_ref, q_ref, kn_ref, vn_ref, kc_ref, vc_ref, gain_ref, normed_ref, resid_ref, wide_gain):
    total = q_ref.shape[0]
    part = total // KV_HEADS
    cached = kc_ref.shape[0]
    for r in range(rows):
        wide_gain[pl.ds(r, total // rows, stride=rows), :] = gain_ref[...]
    scale = HEAD ** -0.5
    scores = jnp.concatenate(
        [
            lax.dot_general(
                q_ref[k * part : (k + 1) * part, :],
                kc_ref[:, k * HEAD : (k + 1) * HEAD],
                (((1,), (1,)), ((), ())),
                preferred_element_type=F32,
            )
            for k in range(KV_HEADS)
        ],
        0,
    ) * scale
    seen = lax.broadcasted_iota(jnp.int32, (total, cached), 1) < len_ref[0]
    scores = jnp.where(seen, scores, -1e30)
    turn = lax.broadcasted_iota(jnp.int32, (total, 1), 0) % rows
    query = q_ref[...].astype(F32)
    fresh = []
    values = []
    for t in range(rows):
        keys = jnp.concatenate(
            [
                jnp.broadcast_to(kn_ref[t : t + 1, k * HEAD : (k + 1) * HEAD].astype(F32), (part, HEAD))
                for k in range(KV_HEADS)
            ],
            0,
        )
        score = jnp.sum(query * keys, axis=1, keepdims=True) * scale
        fresh.append(jnp.where(turn >= t, score, -1e30))
        values.append(
            jnp.concatenate(
                [
                    jnp.broadcast_to(vn_ref[t : t + 1, k * HEAD : (k + 1) * HEAD].astype(F32), (part, HEAD))
                    for k in range(KV_HEADS)
                ],
                0,
            )
        )
    top = jnp.max(scores, axis=1, keepdims=True)
    for score in fresh:
        top = jnp.maximum(top, score)
    raised = jnp.exp(scores - top)
    bottom = jnp.sum(raised, axis=1, keepdims=True)
    lifted = [jnp.exp(score - top) for score in fresh]
    for value in lifted:
        bottom = bottom + value
    probs = (raised / bottom).astype(BF16)
    context = jnp.concatenate(
        [
            jnp.dot(
                probs[k * part : (k + 1) * part, :],
                vc_ref[:, k * HEAD : (k + 1) * HEAD],
                preferred_element_type=F32,
            )
            for k in range(KV_HEADS)
        ],
        0,
    )
    for value, column in zip(lifted, values):
        context = context + (value / bottom).astype(BF16).astype(F32) * column
    resid = hid_ref[...].astype(F32) + context.astype(BF16).astype(F32)
    resid_ref[...] = resid
    square = jnp.sum(resid * resid, axis=1, keepdims=True)
    factor = jnp.zeros((total, 1), F32)
    width = total // rows * HEAD
    for r in range(rows):
        mean = jnp.sum(jnp.where(turn == r, square, 0.0), axis=0, keepdims=True) / width
        factor = jnp.where(turn == r, lax.rsqrt(mean + 1e-05), factor)
    normed_ref[...] = (resid * factor * wide_gain[...]).astype(BF16)


def attend(rows, lengths, hidden, query, key_new, value_new, key_cache, value_cache, gain):
    vmem = pl.BlockSpec(memory_space=VMEM)
    return pl.pallas_call(
        functools.partial(attend_kernel, rows),
        out_shape=(
            VMEM(hidden.shape, BF16),
            VMEM(hidden.shape, F32),
        ),
        in_specs=[vmem, pl.BlockSpec(memory_space=SMEM)] + [vmem] * 7,
        out_specs=(vmem, vmem),
        scratch_shapes=[VMEM(hidden.shape, F32)],
        compiler_params=pltpu.CompilerParams(vmem_limit_bytes=8 << 20),
        name="attend",
    )(first(), lengths, hidden, query, key_new, value_new, key_cache, value_cache, gain)


def pass_kernel(carry_ref, passed_ref):
    passed_ref[...] = carry_ref[...]


def hand_on(carry):
    vmem = pl.BlockSpec(memory_space=VMEM)
    return pl.pallas_call(
        pass_kernel,
        out_shape=VMEM(carry.shape, carry.dtype),
        in_specs=[vmem],
        out_specs=vmem,
        cost_estimate=pl.CostEstimate(flops=20_000_000_000, bytes_accessed=0, transcendentals=0),
        compiler_params=pltpu.CompilerParams(vmem_limit_bytes=4 << 20),
        name="hand_on",
    )(carry)


def join_kernel(*refs):
    for at, ref in enumerate(refs[:-1]):
        refs[-1][:, at] = ref[...]


def join(parts):
    vmem = pl.BlockSpec(memory_space=VMEM)
    return pl.pallas_call(
        join_kernel,
        out_shape=VMEM((parts[0].shape[0], len(parts), *parts[0].shape[1:]), parts[0].dtype),
        in_specs=[vmem] * len(parts),
        out_specs=vmem,
        compiler_params=pltpu.CompilerParams(vmem_limit_bytes=4 << 20),
        name="join",
    )(*parts)


CHUNK = 1024


def hidden_rows(new, width, first, x_ref, table_ref, gate_ref, up_ref):
    rows, depth = x_ref.shape
    units = gate_ref.shape[1]
    gate = jnp.zeros((rows, units), F32)
    upper = jnp.zeros((rows, units), F32)
    for at in range(0, depth, CHUNK):
        block = x_ref[:, at : at + CHUNK]
        gate += jnp.dot(block, gate_ref[at : at + CHUNK, :], preferred_element_type=F32)
        upper += jnp.dot(block, up_ref[at : at + CHUNK, :], preferred_element_type=F32)
    hidden = gate / (1.0 + jnp.exp(-gate)) * upper
    members = width // GROUPS
    chips = members // 2
    me = lax.axis_index("wide")
    block = first + lax.broadcasted_iota(jnp.int32, (rows, width), 0) // new
    group, chip = block % members // chips, block % chips
    source = me ^ (block // members) ^ (group * (members + 1)) ^ (chip * 2 + (chip > 0).astype(jnp.int32))
    column = lax.broadcasted_iota(jnp.int32, (rows, width), 1)
    served = (source == column) & (table_ref[...] == me // members)
    keep = jnp.sum(served.astype(jnp.int32), axis=1, keepdims=True) > 0
    return jnp.where(keep, hidden, 0.0).astype(BF16)


def down_rows(hidden, down_ref, out_ref):
    for at in range(0, out_ref.shape[1], CHUNK):
        out_ref[:, at : at + CHUNK] = jnp.dot(
            hidden, down_ref[:, at : at + CHUNK], preferred_element_type=F32
        ).astype(BF16)


def hidden_kernel(new, width, first, x_ref, table_ref, gate_ref, up_ref, down_ref, out_ref):
    out_ref[...] = hidden_rows(new, width, first, x_ref, table_ref, gate_ref, up_ref)


def feed_kernel(new, width, first, after_ref, x_ref, table_ref, gate_ref, up_ref, down_ref, out_ref):
    down_rows(hidden_rows(new, width, first, x_ref, table_ref, gate_ref, up_ref), down_ref, out_ref)


def down_kernel(after_ref, hidden_ref, down_ref, out_ref):
    down_rows(hidden_ref[...], down_ref, out_ref)


def here(kernel, out_shape, products, name, *operands):
    vmem = pl.BlockSpec(memory_space=VMEM)
    return pl.pallas_call(
        kernel,
        out_shape=VMEM(out_shape, BF16),
        in_specs=[vmem] * len(operands),
        out_specs=vmem,
        compiler_params=pltpu.CompilerParams(vmem_limit_bytes=16 << 20),
        cost_estimate=pl.CostEstimate(flops=2 * products, bytes_accessed=0, transcendentals=0),
        name=name,
    )(*[pltpu.with_memory_space_constraint(x, VMEM) for x in operands])


def swap(x, bits, width):
    return lax.ppermute(x, "wide", [(i, i ^ bits) for i in range(width)])


def local(
    hidden_in,
    queries,
    key_new,
    value_new,
    key_cache,
    value_cache,
    lengths,
    table,
    gain,
    gate_weight,
    up_weight,
    down_weight,
):
    rows, depth = hidden_in.shape
    blocks = depth // HEAD
    width = lax.axis_size("wide")
    members = width // GROUPS
    chips = members // 2

    def pairs(x):
        return x.reshape(rows, blocks, HEAD).transpose(1, 0, 2).reshape(rows * blocks, HEAD)

    normed, resid = attend(
        rows,
        lengths,
        pairs(hidden_in),
        pairs(queries),
        key_new,
        value_new,
        key_cache,
        value_cache,
        gain.reshape(blocks, HEAD),
    )
    twin = swap(normed, members + 1, width)
    normed = hand_on(normed)
    both = jnp.stack([normed, twin], 0)
    came = [swap(both, 2 * k + 1, width) for k in range(1, chips)]
    mine = join([both] + came).reshape(members, blocks, rows, HEAD).transpose(0, 2, 1, 3).reshape(members * rows, depth)
    other = swap(mine, 1, width)
    table = table.reshape(1, width)
    units = gate_weight.shape[1]
    size = members * rows * depth * units
    hidden = here(
        functools.partial(hidden_kernel, rows, width, 0),
        (members * rows, units), 0, "feed_own", mine, table, gate_weight, up_weight, down_weight,
    )
    sent = here(
        functools.partial(feed_kernel, rows, width, members),
        mine.shape, 3 * size, "feed_other", hidden, other, table, gate_weight, up_weight, down_weight,
    )
    came = swap(sent, 1, width)
    kept = here(down_kernel, mine.shape, size, "down_own", sent, hidden, down_weight)
    summed = kept.astype(F32) + came.astype(F32)
    half = chips * rows

    forward = list(range(1, chips))

    def gather(first, order):
        total = summed[first : first + rows]
        for k in order:
            at = first + k * rows
            total = total + swap(summed[at : at + rows].astype(BF16), 2 * k + 1, width).astype(F32)
        return total

    other = swap(gather(half, forward).astype(BF16), members + 1, width)
    ffn_out = (gather(0, forward[::-1]) + other.astype(F32)).astype(BF16).astype(F32)
    resid = resid.reshape(blocks, rows, HEAD).transpose(1, 0, 2).reshape(rows, depth)
    return (resid + ffn_out).astype(BF16)


def solution(mesh):
    in_specs = (
        P(("parts", "wide"), None),
        P(("parts", "wide"), None),
        P(("parts", "wide"), None),
        P(("parts", "wide"), None),
        P(("parts", "wide"), None),
        P(("parts", "wide"), None),
        P(("parts", "wide")),
        P("parts", None),
        P(),
        P(None, "wide"),
        P(None, "wide"),
        P("wide", None),
    )
    out_specs = P(("parts", "wide"), None)
    return jax.shard_map(local, mesh=mesh, in_specs=in_specs, out_specs=out_specs, check_vma=False)
```
